32 devices in a mesh: blk: 8 (over y, x, core), narrow: 4 (over z).
Axes of the slice: x: 2, y: 2, z: 4, core: 2. Of those that a mesh axis runs over, the one named last changes fastest.
Arguments:
- codes: bfloat16 [6144, 12288], P(('blk', 'narrow')), may hold values from -6 to 6
- signals: bfloat16 [6144, 192], P(('blk', 'narrow')), may hold values from -6 to 6
- dictionary: bfloat16 [12288, 192], P('blk'), may hold values from -0.0546875 to 0.0546875
Outputs:
- new_codes: bfloat16 [6144, 12288], P(('blk', 'narrow'))
- dict_grad: float32 [12288, 192], P(('blk', 'narrow'))
The draws below stay inside these ranges and needn't reach their ends.
All inputs are finite; a program needn't handle non-finite values.
Results may differ from the reference program's by a relative error of at most 0.0095.
Values may be sent and summed in bfloat16 or wider, within the bound.
A program may use at most 64 MiB of HBM per device.

```python
import jax
import jax.numpy as jnp
from jax import lax

F = 192
K = 12288
NB = 6144
N_BLK = 8


def raised(array, own_key, source, target, shards_of, factor):
    owner, partner = [(jnp.arange(array.shape[axis_at]) // (array.shape[axis_at] // shards_of)).reshape([-1 if axis == axis_at else 1 for axis in range(array.ndim)]) for axis_at in (source, target)]
    chosen = jax.random.permutation(own_key, shards_of)[partner]
    strong = (owner == chosen) | (owner == (partner + shards_of // 2) % shards_of)
    return jnp.where(strong, factor * array, array)


def shard_levels(key, dims, cuts, least, largest):
    def one(dim, shards_of):
        draws = jax.random.uniform(jax.random.fold_in(jax.random.fold_in(key, 6), dim), (shards_of,), jnp.float32, least / len(cuts), largest / len(cuts))
        return jnp.repeat(jnp.exp(draws), dims[dim] // shards_of).reshape((-1,) + (1,) * (len(dims) - dim - 1))

    factor_of = one(*cuts[0])
    for cut in cuts[1:]:
        factor_of = factor_of * one(*cut)
    return factor_of


def centred(own_key, shape, deviation, reach, split=(), dtype=jnp.bfloat16):
    gain = shard_levels(own_key, shape, split, -0.22, 0.18) if split else 1.0
    result = jax.random.normal(own_key, shape, jnp.float32) * deviation * gain
    return jnp.minimum(jnp.maximum(result, -reach), reach).astype(dtype)


def noise_with(own_key, dims, width, reach, split, heavy, kind=jnp.bfloat16):
    drawn = width * jax.random.normal(own_key, dims, jnp.float32)
    if split:
        drawn = drawn * shard_levels(own_key, dims, split, -0.22, 0.18)
    return jnp.clip(raised(drawn, jax.random.fold_in(own_key, 3), *heavy), -reach, reach).astype(kind)


def setup_inputs(seed: int = 0) -> dict:
    seeds = jax.random.split(jax.random.key(seed), 4)
    return {
        "codes": noise_with(seeds[0], (NB, K), 1.0, 6.0, ((0, 32),), (0, 1, 32, 2.75)),
        "signals": centred(seeds[1], (NB, F), 1.0, 6.0, ((0, 32),)),
        "dictionary": centred(seeds[2], (K, F), K ** -0.5, 0.0546875, ((0, 8),)),
    }


def shrink(values):
    return jnp.sign(values) * jnp.maximum(jnp.abs(values) - 0.5, 0.0)


def reference(codes, signals, dictionary):
    total_rows = codes.shape[0]
    block_rows = total_rows // N_BLK
    block_count = N_BLK
    code_blocks = codes.reshape(block_count, block_rows, codes.shape[1])
    signal_blocks = signals.reshape(block_count, block_rows, signals.shape[1])

    def one_block(pair):
        code_part, signal_part = pair
        estimate = jnp.dot(code_part, dictionary, preferred_element_type=jnp.float32)
        misfit = (estimate - signal_part.astype(jnp.float32)).astype(jnp.bfloat16)
        correlation = lax.dot_general(misfit, dictionary, (((1,), (1,)), ((), ())), preferred_element_type=jnp.float32)
        fresh = shrink(code_part.astype(jnp.float32) - 4.0 * correlation).astype(jnp.bfloat16)
        second = jnp.dot(fresh, dictionary, preferred_element_type=jnp.float32)
        misfit_two = (second - signal_part.astype(jnp.float32)).astype(jnp.bfloat16)
        return fresh, misfit_two

    fresh_blocks, misfit_blocks = lax.map(one_block, (code_blocks, signal_blocks))
    new_codes = fresh_blocks.reshape(total_rows, codes.shape[1])
    misfit_two = misfit_blocks.reshape(total_rows, signals.shape[1])
    dict_grad = lax.dot_general(new_codes, misfit_two, (((0,), (0,)), ((), ())), preferred_element_type=jnp.float32)
    return new_codes, dict_grad * (float(total_rows) ** -0.5)
```

```python
import functools

import jax
import jax.numpy as jnp
from jax import lax
from jax.experimental import pallas as pl
from jax.experimental.pallas import tpu as pltpu
from jax.sharding import PartitionSpec as P

MESH = pl.DeviceIdType.MESH
VMEM = pltpu.VMEM
DMA = pltpu.SemaphoreType.DMA
HALVES = 2
CORES = 2


def flip(chip, distance):
    bit = 1
    while bit <= distance:
        if distance & bit:
            chip = chip + bit * (1 - 2 * ((chip // bit) % 2))
        bit *= 2
    return chip


def low(d):
    return d & -d


def high(d):
    return 1 << (d.bit_length() - 1)


def ones(d):
    return bin(d).count("1")


def bits_of(chips):
    return [1 << i for i in range(chips.bit_length() - 1)]


def toward(d, half):
    return low(d) if half == 0 else high(d)


def children(d, half, bits):
    return [b for b in bits if d == 0 or (b < low(d) if half == 0 else b > high(d))]


def pieces_of(chips):
    return [(d, h) for d in range(chips) for h in range(HALVES)]


def nt_dot(a, b):
    return lax.dot_general(a, b, (((1,), (1,)), ((), ())), preferred_element_type=jnp.float32)


def gather_kernel(
    chips, codes, signals, atoms, full, misfit, held, total,
    load_sem, atom_sem, net_send, net_recv, core_send, core_recv,
):
    bits = bits_of(chips)
    me = lax.axis_index("blk")
    chip, core = me // CORES, me % CORES
    other = CORES * chip + 1 - core
    width = full.shape[2]

    def owner(d, c):
        return CORES * flip(chip, d) + c

    order = sorted(
        pieces_of(chips),
        key=lambda p: (ones(p[0]), -len(children(p[0], p[1], bits)), p[0]),
    )
    uses = [(d, h, c) for d, h in order for c in range(CORES)]

    def atom_copy(h):
        return pltpu.make_async_copy(
            atoms.at[:, pl.ds(h * width, width)], full.at[me * HALVES + h], atom_sem.at[h]
        )

    def block(d, h, c):
        return owner(d, core if c == 0 else 1 - core) * HALVES + h

    def load(slot):
        d, h, c = uses[slot]
        start = pl.multiple_of(block(d, h, c) * width, width)
        return pltpu.make_async_copy(
            codes.at[:, pl.ds(start, width)], held.at[slot], load_sem.at[slot]
        )

    for h in range(HALVES):
        atom_copy(h).start()
    partners = [other] + [CORES * flip(chip, b) + core for b in bits]
    barrier = pltpu.get_barrier_semaphore()
    for partner in partners:
        pl.semaphore_signal(barrier, inc=1, device_id={"blk": partner}, device_id_type=MESH)
    for slot in range(len(uses)):
        load(slot).start()

    sends = []

    def net(d, h, b):
        place = full.at[block(d, h, 0)]
        copy = pltpu.make_async_remote_copy(
            place, place, net_send.at[len(sends)], net_recv.at[(d ^ b) * HALVES + h],
            device_id={"blk": CORES * flip(chip, b) + core}, device_id_type=MESH,
        )
        copy.start()
        sends.append(copy)

    def across(d, h, c):
        place = full.at[block(d, h, c)]
        index = d * HALVES + h
        return pltpu.make_async_remote_copy(
            place, place, core_send.at[index], core_recv.at[index],
            device_id={"blk": other}, device_id_type=MESH,
        )

    def arrived(d, h):
        place = full.at[block(d, h, 0)]
        pltpu.make_async_remote_copy(
            place, place, net_send.at[0], net_recv.at[d * HALVES + h],
            device_id={"blk": other}, device_id_type=MESH,
        ).wait_recv()

    def use(d, h, c):
        slot = uses.index((d, h, c))
        load(slot).wait()
        total[...] += nt_dot(held[slot], full[block(d, h, c)])

    for h in range(HALVES):
        atom_copy(h).wait()
    pl.semaphore_wait(barrier, len(partners))
    for step in range(HALVES):
        for i, b in enumerate(bits):
            h = 1 - step if i == 0 else step
            net(0, h, b)
        across(0, step, 0).start()
    total[...] = jnp.zeros_like(total)
    waiting = []
    for d, h in order:
        if d:
            arrived(d, h)
            for b in children(d, h, bits):
                net(d, h, b)
            across(d, h, 0).start()
        use(d, h, 0)
        waiting.append((d, h))
        if len(waiting) > 1:
            e, k = waiting.pop(0)
            across(e, k, 1).wait_recv()
            use(e, k, 1)
    for e, k in waiting:
        across(e, k, 1).wait_recv()
        use(e, k, 1)
    rounded = (total[...] - signals[...].astype(jnp.float32)).astype(jnp.bfloat16)
    misfit[...] = (rounded.astype(jnp.float32) * -4.0).astype(jnp.bfloat16)
    for copy in sends:
        copy.wait_send()
    for d, h in order:
        across(d, h, 0).wait_send()


def update_kernel(codes, signals, full, misfit, fresh, misfit_two, total):
    step = pl.program_id(0)

    @pl.when(step == 0)
    def _():
        total[...] = jnp.zeros_like(total)

    change = jnp.dot(misfit[...], full[0], preferred_element_type=jnp.float32)
    moved = codes[...].astype(jnp.float32) + change
    shrunk = (moved - jnp.clip(moved, -0.5, 0.5)).astype(jnp.bfloat16)
    fresh[...] = shrunk
    total[...] += nt_dot(shrunk, full[0])

    @pl.when(step == pl.num_programs(0) - 1)
    def _():
        left = total[...] - signals[...].astype(jnp.float32)
        misfit_two[...] = left.T.astype(jnp.bfloat16)


def gradient_kernel(
    chips, line, scale, fresh, misfit, grad,
    held, core_out, core_in, net_out, net_in, own, z_out, z_in,
    load_sem, core_send, core_recv, net_send, net_recv, z_send, z_recv,
):
    bits = bits_of(chips)
    me = lax.axis_index("blk")
    z = lax.axis_index("narrow")
    chip, core = me // CORES, me % CORES
    other = CORES * chip + 1 - core
    width = held.shape[2]
    part = grad.shape[1]

    order = sorted(
        pieces_of(chips),
        key=lambda p: (-ones(p[0]), len(children(p[0], p[1], bits)), p[0]),
    )
    uses = [(d, h, c) for d, h in order for c in (1, 0)]
    entries = [(d, h, b) for d, h in order for b in children(d, h, bits)]

    def load(slot):
        d, h, c = uses[slot]
        owner = CORES * flip(chip, d) + (core if c == 0 else 1 - core)
        start = pl.multiple_of((owner * HALVES + h) * width, width)
        return pltpu.make_async_copy(
            fresh.at[:, pl.ds(start, width)], held.at[slot], load_sem.at[slot]
        )

    for slot in range(len(uses)):
        load(slot).start()
    barrier = pltpu.get_barrier_semaphore()
    partners = [other] + [CORES * flip(chip, b) + core for b in bits]
    for partner in partners:
        pl.semaphore_signal(barrier, inc=1, device_id={"blk": partner}, device_id_type=MESH)
    beside = [(z + 1) % line, (z + line - 1) % line] if line > 1 else []
    for partner in beside:
        pl.semaphore_signal(barrier, inc=1, device_id={"narrow": partner}, device_id_type=MESH)

    def term(d, h, c):
        slot = uses.index((d, h, c))
        load(slot).wait()
        return jnp.dot(misfit[...], held[slot], preferred_element_type=jnp.float32)

    def across(i):
        return pltpu.make_async_remote_copy(
            core_out.at[i], core_in.at[i], core_send.at[i], core_recv.at[i],
            device_id={"blk": other}, device_id_type=MESH,
        )

    def net(i, slot, b):
        return pltpu.make_async_remote_copy(
            net_out.at[i], net_in.at[slot], net_send.at[i], net_recv.at[slot],
            device_id={"blk": CORES * flip(chip, b) + core}, device_id_type=MESH,
        )

    def hand_over(i):
        d, h = order[i]
        core_out[i] = term(d, h, 1).astype(jnp.bfloat16)
        if i == 0:
            pl.semaphore_wait(barrier, len(partners) + len(beside))
        across(i).start()

    ahead = min(2, len(order))
    for i in range(ahead):
        hand_over(i)
    sends = []
    for i, (d, h) in enumerate(order):
        if i + ahead < len(order):
            hand_over(i + ahead)
        value = term(d, h, 0)
        across(i).wait_recv()
        value += core_in[i].astype(jnp.float32)
        for b in children(d, h, bits):
            slot = entries.index((d, h, b))
            net(0, slot, b).wait_recv()
            value += net_in[slot].astype(jnp.float32)
        if d:
            b = toward(d, h)
            net_out[i] = value.astype(jnp.bfloat16)
            copy = net(i, entries.index((d ^ b, h, b)), b)
            copy.start()
            sends.append(copy)
        else:
            for j in range(width // part):
                own[h * (width // part) + j] = value[:, j * part:(j + 1) * part]

    def z_copy(side, t):
        return pltpu.make_async_remote_copy(
            z_out.at[side, t], z_in.at[side, t - 1],
            z_send.at[side, t], z_recv.at[side, t - 1],
            device_id={"narrow": z + 1 if side == 0 else z - 1}, device_id_type=MESH,
        )

    def z_arrived(side, t):
        pltpu.make_async_remote_copy(
            z_out.at[side, 0], z_in.at[side, t], z_send.at[side, 0], z_recv.at[side, t],
            device_id={"narrow": z - 1 if side == 0 else z + 1}, device_id_type=MESH,
        ).wait_recv()

    def has_behind(side):
        return z >= 1 if side == 0 else z <= line - 2

    def in_line(side, t):
        return z + t < line if side == 0 else z - t >= 0

    for t in range(line - 1, 0, -1):
        for side in range(2):
            @pl.when(in_line(side, t))
            def _():
                mine = own[z + t if side == 0 else z - t]

                @pl.when(has_behind(side))
                def _():
                    z_arrived(side, t)
                    z_out[side, t] = (mine + z_in[side, t].astype(jnp.float32)).astype(jnp.bfloat16)

                @pl.when(jnp.logical_not(has_behind(side)))
                def _():
                    z_out[side, t] = mine.astype(jnp.bfloat16)

                z_copy(side, t).start()

    grad[...] = own[z]
    if line > 1:
        for side in range(2):
            @pl.when(has_behind(side))
            def _():
                z_arrived(side, 0)
                grad[...] += z_in[side, 0].astype(jnp.float32)
    grad[...] = grad[...] * scale

    for t in range(line - 1, 0, -1):
        for side in range(2):
            @pl.when(in_line(side, t))
            def _():
                z_copy(side, t).wait_send()
    for copy in sends:
        copy.wait_send()
    for i in range(len(order)):
        across(i).wait_send()


def body(blk, line, codes, signals, dictionary):
    rows, count = codes.shape
    atoms, features = dictionary.shape
    chips = blk // CORES
    width = atoms // HALVES
    blocks = blk * HALVES
    pieces = chips * HALVES
    links = len(bits_of(chips))
    part = atoms // line
    bf16, f32 = jnp.bfloat16, jnp.float32
    any_spec = pl.BlockSpec(memory_space=pl.ANY)
    vmem_spec = pl.BlockSpec(memory_space=VMEM)
    flops = 2 * rows * count * features
    size = 2 * rows * count

    full, misfit = pl.pallas_call(
        functools.partial(gather_kernel, chips),
        out_shape=(
            jax.ShapeDtypeStruct((blocks, features, width), bf16),
            jax.ShapeDtypeStruct((rows, features), bf16),
        ),
        in_specs=[any_spec, vmem_spec, any_spec],
        out_specs=(vmem_spec, vmem_spec),
        scratch_shapes=[
            VMEM((blocks, rows, width), bf16),
            VMEM((rows, features), f32),
            DMA((blocks,)), DMA((HALVES,)),
            DMA((HALVES * max(chips - 1, 1),)), DMA((pieces,)),
            DMA((pieces,)), DMA((pieces,)),
        ],
        compiler_params=pltpu.CompilerParams(
            collective_id=0, has_side_effects=True, vmem_limit_bytes=32 * 2**20
        ),
        cost_estimate=pl.CostEstimate(flops=flops, bytes_accessed=2 * size, transcendentals=0),
        name="gather_atoms",
    )(codes, signals, dictionary.T)

    fresh, misfit_two = pl.pallas_call(
        update_kernel,
        grid=(blocks,),
        out_shape=(
            jax.ShapeDtypeStruct((rows, count), bf16),
            jax.ShapeDtypeStruct((features, rows), bf16),
        ),
        in_specs=[
            pl.BlockSpec((rows, width), lambda i: (0, i)),
            pl.BlockSpec((rows, features), lambda i: (0, 0)),
            pl.BlockSpec((1, features, width), lambda i: (i, 0, 0)),
            pl.BlockSpec((rows, features), lambda i: (0, 0)),
        ],
        out_specs=(
            pl.BlockSpec((rows, width), lambda i: (0, i)),
            pl.BlockSpec((features, rows), lambda i: (0, 0)),
        ),
        scratch_shapes=[VMEM((rows, features), f32)],
        compiler_params=pltpu.CompilerParams(vmem_limit_bytes=24 * 2**20),
        cost_estimate=pl.CostEstimate(flops=2 * flops, bytes_accessed=3 * size, transcendentals=0),
        name="update_codes",
    )(codes, signals, full, misfit)

    grad = pl.pallas_call(
        functools.partial(gradient_kernel, chips, line, float(rows * blk * line) ** -0.5),
        out_shape=jax.ShapeDtypeStruct((features, part), f32),
        in_specs=[any_spec, vmem_spec],
        out_specs=vmem_spec,
        scratch_shapes=[
            VMEM((blocks, rows, width), bf16),
            VMEM((pieces, features, width), bf16),
            VMEM((pieces, features, width), bf16),
            VMEM((pieces, features, width), bf16),
            VMEM((max(HALVES * (chips - 1), 1), features, width), bf16),
            VMEM((line, features, part), f32),
            VMEM((2, line, features, part), bf16),
            VMEM((2, line, features, part), bf16),
            DMA((blocks,)), DMA((pieces,)), DMA((pieces,)), DMA((pieces,)),
            DMA((max(HALVES * (chips - 1), 1),)), DMA((2, line)), DMA((2, line)),
        ],
        compiler_params=pltpu.CompilerParams(
            collective_id=1, has_side_effects=True, vmem_limit_bytes=40 * 2**20
        ),
        cost_estimate=pl.CostEstimate(flops=flops, bytes_accessed=2 * size, transcendentals=0),
        name="dictionary_gradient",
    )(fresh, misfit_two)
    return fresh, grad.T


def solution(mesh):
    placed = (P(("blk", "narrow"), None), P(("blk", "narrow"), None), P("blk", None))
    return jax.shard_map(
        functools.partial(body, mesh.shape["blk"], mesh.shape["narrow"]),
        mesh=mesh,
        in_specs=placed,
        out_specs=(P(("blk", "narrow"), None), P(("blk", "narrow"), None)),
        check_vma=False,
    )
```

```python
import functools

import jax
import jax.numpy as jnp
from jax import lax
from jax.experimental import pallas as pl
from jax.experimental.pallas import tpu as pltpu
from jax.sharding import PartitionSpec as P

MESH = pl.DeviceIdType.MESH
VMEM = pltpu.VMEM
DMA = pltpu.SemaphoreType.DMA
HALVES = 2
CORES = 2


def flip(chip, distance):
    bit = 1
    while bit <= distance:
        if distance & bit:
            chip = chip + bit * (1 - 2 * ((chip // bit) % 2))
        bit *= 2
    return chip


def low(d):
    return d & -d


def high(d):
    return 1 << (d.bit_length() - 1)


def ones(d):
    return bin(d).count("1")


def bits_of(chips):
    return [1 << i for i in range(chips.bit_length() - 1)]


def toward(d, half):
    return low(d) if half == 0 else high(d)


def children(d, half, bits):
    return [b for b in bits if d == 0 or (b < low(d) if half == 0 else b > high(d))]


def pieces_of(chips):
    return [(d, h) for d in range(chips) for h in range(HALVES)]


def nt_dot(a, b):
    return lax.dot_general(a, b, (((1,), (1,)), ((), ())), preferred_element_type=jnp.float32)


def gather_kernel(
    chips, codes, signals, atoms, full, misfit, held, target, total,
    load_sem, target_sem, atom_sem, net_send, net_recv, core_send, core_recv,
):
    bits = bits_of(chips)
    me = lax.axis_index("blk")
    chip, core = me // CORES, me % CORES
    other = CORES * chip + 1 - core
    width = full.shape[2]

    def owner(d, c):
        return CORES * flip(chip, d) + c

    order = sorted(
        pieces_of(chips),
        key=lambda p: (ones(p[0]), -len(children(p[0], p[1], bits)), p[0]),
    )
    uses = [(d, h, c) for d, h in order for c in range(CORES)]

    def atom_copy(h):
        return pltpu.make_async_copy(
            atoms.at[:, pl.ds(h * width, width)], full.at[me * HALVES + h], atom_sem.at[h]
        )

    def block(d, h, c):
        return owner(d, core if c == 0 else 1 - core) * HALVES + h

    def load(slot):
        d, h, c = uses[slot]
        start = pl.multiple_of(block(d, h, c) * width, width)
        return pltpu.make_async_copy(
            codes.at[:, pl.ds(start, width)], held.at[slot], load_sem.at[slot]
        )

    for h in range(HALVES):
        atom_copy(h).start()
    partners = [other] + [CORES * flip(chip, b) + core for b in bits]
    barrier = pltpu.get_barrier_semaphore()
    for partner in partners:
        pl.semaphore_signal(barrier, inc=1, device_id={"blk": partner}, device_id_type=MESH)
    for slot in range(len(uses)):
        load(slot).start()

    target_copy = pltpu.make_async_copy(signals, target, target_sem)
    target_copy.start()

    sends = []

    def net(d, h, b):
        place = full.at[block(d, h, 0)]
        copy = pltpu.make_async_remote_copy(
            place, place, net_send.at[len(sends)], net_recv.at[(d ^ b) * HALVES + h],
            device_id={"blk": CORES * flip(chip, b) + core}, device_id_type=MESH,
        )
        copy.start()
        sends.append(copy)

    def across(d, h, c):
        place = full.at[block(d, h, c)]
        index = d * HALVES + h
        return pltpu.make_async_remote_copy(
            place, place, core_send.at[index], core_recv.at[index],
            device_id={"blk": other}, device_id_type=MESH,
        )

    def arrived(d, h):
        place = full.at[block(d, h, 0)]
        pltpu.make_async_remote_copy(
            place, place, net_send.at[0], net_recv.at[d * HALVES + h],
            device_id={"blk": other}, device_id_type=MESH,
        ).wait_recv()

    def use(d, h, c):
        slot = uses.index((d, h, c))
        load(slot).wait()
        total[...] += nt_dot(held[slot], full[block(d, h, c)])

    for h in range(HALVES):
        atom_copy(h).wait()
    pl.semaphore_wait(barrier, len(partners))
    for step in range(HALVES):
        for i, b in enumerate(bits):
            h = 1 - step if i == 0 else step
            net(0, h, b)
        across(0, step, 0).start()
    total[...] = jnp.zeros_like(total)
    waiting = []
    for d, h in order:
        if d:
            arrived(d, h)
            for b in children(d, h, bits):
                net(d, h, b)
            across(d, h, 0).start()
        use(d, h, 0)
        waiting.append((d, h))
        if len(waiting) > 1:
            e, k = waiting.pop(0)
            across(e, k, 1).wait_recv()
            use(e, k, 1)
    for e, k in waiting:
        across(e, k, 1).wait_recv()
        use(e, k, 1)
    target_copy.wait()
    rounded = (total[...] - target[...].astype(jnp.float32)).astype(jnp.bfloat16)
    misfit[...] = (rounded.astype(jnp.float32) * -4.0).astype(jnp.bfloat16)
    for copy in sends:
        copy.wait_send()
    for d, h in order:
        across(d, h, 0).wait_send()


def update_kernel(together, codes, signals, full, misfit, fresh, misfit_two, made, total, store_sem):
    blocks, _, width = full.shape

    def store(i):
        start = pl.multiple_of(i * width, width)
        return pltpu.make_async_copy(
            made.at[i], fresh.at[:, pl.ds(start, width)], store_sem.at[i]
        )

    total[...] = jnp.zeros_like(total)

    @pl.loop(0, blocks // together)
    def _(step):
        for j in range(together):
            i = step * together + j
            start = pl.multiple_of(i * width, width)
            change = jnp.dot(misfit[...], full[i], preferred_element_type=jnp.float32)
            moved = codes[:, pl.ds(start, width)].astype(jnp.float32) + change
            made[i] = (moved - jnp.clip(moved, -0.5, 0.5)).astype(jnp.bfloat16)
            store(i).start()
        for j in range(together):
            i = step * together + j
            total[...] += nt_dot(made[i], full[i])

    left = total[...] - signals[...].astype(jnp.float32)
    misfit_two[...] = left.T.astype(jnp.bfloat16)
    for i in range(blocks):
        store(i).wait()


def gradient_kernel(
    chips, line, scale, fresh, misfit, grad,
    held, core_out, core_in, net_out, net_in, own, z_out, z_in,
    load_sem, core_send, core_recv, net_send, net_recv, z_send, z_recv,
):
    bits = bits_of(chips)
    me = lax.axis_index("blk")
    z = lax.axis_index("narrow")
    chip, core = me // CORES, me % CORES
    other = CORES * chip + 1 - core
    width = held.shape[2]
    part = grad.shape[1]

    order = sorted(
        pieces_of(chips),
        key=lambda p: (-ones(p[0]), len(children(p[0], p[1], bits)), p[0]),
    )
    uses = [(d, h, c) for d, h in order for c in (1, 0)]
    entries = [(d, h, b) for d, h in order for b in children(d, h, bits)]

    def load(slot):
        d, h, c = uses[slot]
        owner = CORES * flip(chip, d) + (core if c == 0 else 1 - core)
        start = pl.multiple_of((owner * HALVES + h) * width, width)
        return pltpu.make_async_copy(
            fresh.at[:, pl.ds(start, width)], held.at[slot], load_sem.at[slot]
        )

    for slot in range(len(uses)):
        load(slot).start()
    barrier = pltpu.get_barrier_semaphore()
    partners = [other] + [CORES * flip(chip, b) + core for b in bits]
    for partner in partners:
        pl.semaphore_signal(barrier, inc=1, device_id={"blk": partner}, device_id_type=MESH)
    beside = [(z + 1) % line, (z + line - 1) % line] if line > 1 else []
    for partner in beside:
        pl.semaphore_signal(barrier, inc=1, device_id={"narrow": partner}, device_id_type=MESH)

    def term(d, h, c):
        slot = uses.index((d, h, c))
        load(slot).wait()
        return jnp.dot(misfit[...], held[slot], preferred_element_type=jnp.float32)

    def across(i):
        return pltpu.make_async_remote_copy(
            core_out.at[i], core_in.at[i], core_send.at[i], core_recv.at[i],
            device_id={"blk": other}, device_id_type=MESH,
        )

    def net(i, slot, b):
        return pltpu.make_async_remote_copy(
            net_out.at[i], net_in.at[slot], net_send.at[i], net_recv.at[slot],
            device_id={"blk": CORES * flip(chip, b) + core}, device_id_type=MESH,
        )

    def hand_over(i):
        d, h = order[i]
        core_out[i] = term(d, h, 1).astype(jnp.bfloat16)
        if i == 0:
            pl.semaphore_wait(barrier, len(partners) + len(beside))
        across(i).start()

    ahead = min(2, len(order))
    for i in range(ahead):
        hand_over(i)
    sends = []
    for i, (d, h) in enumerate(order):
        if i + ahead < len(order):
            hand_over(i + ahead)
        value = term(d, h, 0)
        across(i).wait_recv()
        value += core_in[i].astype(jnp.float32)
        for b in children(d, h, bits):
            slot = entries.index((d, h, b))
            net(0, slot, b).wait_recv()
            value += net_in[slot].astype(jnp.float32)
        if d:
            b = toward(d, h)
            net_out[i] = value.astype(jnp.bfloat16)
            copy = net(i, entries.index((d ^ b, h, b)), b)
            copy.start()
            sends.append(copy)
        else:
            for j in range(width // part):
                own[h * (width // part) + j] = value[:, j * part:(j + 1) * part]

    def z_copy(side, t):
        return pltpu.make_async_remote_copy(
            z_out.at[side, t], z_in.at[side, t - 1],
            z_send.at[side, t], z_recv.at[side, t - 1],
            device_id={"narrow": z + 1 if side == 0 else z - 1}, device_id_type=MESH,
        )

    def z_arrived(side, t):
        pltpu.make_async_remote_copy(
            z_out.at[side, 0], z_in.at[side, t], z_send.at[side, 0], z_recv.at[side, t],
            device_id={"narrow": z - 1 if side == 0 else z + 1}, device_id_type=MESH,
        ).wait_recv()

    def has_behind(side):
        return z >= 1 if side == 0 else z <= line - 2

    def in_line(side, t):
        return z + t < line if side == 0 else z - t >= 0

    for t in range(line - 1, 0, -1):
        for side in range(2):
            @pl.when(in_line(side, t))
            def _():
                mine = own[z + t if side == 0 else z - t]

                @pl.when(has_behind(side))
                def _():
                    z_arrived(side, t)
                    z_out[side, t] = (mine + z_in[side, t].astype(jnp.float32)).astype(jnp.bfloat16)

                @pl.when(jnp.logical_not(has_behind(side)))
                def _():
                    z_out[side, t] = mine.astype(jnp.bfloat16)

                z_copy(side, t).start()

    grad[...] = own[z]
    if line > 1:
        for side in range(2):
            @pl.when(has_behind(side))
            def _():
                z_arrived(side, 0)
                grad[...] += z_in[side, 0].astype(jnp.float32)
    grad[...] = grad[...] * scale

    for t in range(line - 1, 0, -1):
        for side in range(2):
            @pl.when(in_line(side, t))
            def _():
                z_copy(side, t).wait_send()
    for copy in sends:
        copy.wait_send()
    for i in range(len(order)):
        across(i).wait_send()


def in_hbm(array):
    return pltpu.with_memory_space_constraint(array, pltpu.HBM)


def body(blk, line, codes, signals, dictionary):
    rows, count = codes.shape
    atoms, features = dictionary.shape
    chips = blk // CORES
    width = atoms // HALVES
    blocks = blk * HALVES
    pieces = chips * HALVES
    links = len(bits_of(chips))
    part = atoms // line
    bf16, f32 = jnp.bfloat16, jnp.float32
    hbm_spec = pl.BlockSpec(memory_space=pltpu.HBM)
    vmem_spec = pl.BlockSpec(memory_space=VMEM)
    flops = 2 * rows * count * features
    size = 2 * rows * count

    full, misfit = pl.pallas_call(
        functools.partial(gather_kernel, chips),
        out_shape=(
            jax.ShapeDtypeStruct((blocks, features, width), bf16),
            jax.ShapeDtypeStruct((rows, features), bf16),
        ),
        in_specs=[hbm_spec] * 3,
        out_specs=(vmem_spec, vmem_spec),
        scratch_shapes=[
            VMEM((blocks, rows, width), bf16),
            VMEM((rows, features), bf16),
            VMEM((rows, features), f32),
            DMA((blocks,)), DMA, DMA((HALVES,)),
            DMA((HALVES * max(chips - 1, 1),)), DMA((pieces,)),
            DMA((pieces,)), DMA((pieces,)),
        ],
        compiler_params=pltpu.CompilerParams(
            collective_id=0, has_side_effects=True, vmem_limit_bytes=32 * 2**20
        ),
        cost_estimate=pl.CostEstimate(flops=flops, bytes_accessed=2 * size, transcendentals=0),
        name="gather_atoms",
    )(in_hbm(codes), in_hbm(signals), in_hbm(dictionary.T))

    fresh, misfit_two = pl.pallas_call(
        functools.partial(update_kernel, 4),
        out_shape=(
            jax.ShapeDtypeStruct((rows, count), bf16),
            jax.ShapeDtypeStruct((features, rows), bf16),
        ),
        in_specs=[vmem_spec] * 4,
        out_specs=(hbm_spec, vmem_spec),
        scratch_shapes=[
            VMEM((blocks, rows, width), bf16),
            VMEM((rows, features), f32),
            DMA((blocks,)),
        ],
        compiler_params=pltpu.CompilerParams(vmem_limit_bytes=24 * 2**20),
        cost_estimate=pl.CostEstimate(flops=2 * flops, bytes_accessed=3 * size, transcendentals=0),
        name="update_codes",
    )(codes, signals, full, misfit)

    grad = pl.pallas_call(
        functools.partial(gradient_kernel, chips, line, float(rows * blk * line) ** -0.5),
        out_shape=jax.ShapeDtypeStruct((features, part), f32),
        in_specs=[hbm_spec, vmem_spec],
        out_specs=vmem_spec,
        scratch_shapes=[
            VMEM((blocks, rows, width), bf16),
            VMEM((pieces, features, width), bf16),
            VMEM((pieces, features, width), bf16),
            VMEM((pieces, features, width), bf16),
            VMEM((max(HALVES * (chips - 1), 1), features, width), bf16),
            VMEM((line, features, part), f32),
            VMEM((2, line, features, part), bf16),
            VMEM((2, line, features, part), bf16),
            DMA((blocks,)), DMA((pieces,)), DMA((pieces,)), DMA((pieces,)),
            DMA((max(HALVES * (chips - 1), 1),)), DMA((2, line)), DMA((2, line)),
        ],
        compiler_params=pltpu.CompilerParams(
            collective_id=1, has_side_effects=True, vmem_limit_bytes=40 * 2**20
        ),
        cost_estimate=pl.CostEstimate(flops=flops, bytes_accessed=2 * size, transcendentals=0),
        name="dictionary_gradient",
    )(in_hbm(fresh), misfit_two)
    return fresh, grad.T


def solution(mesh):
    placed = (P(("blk", "narrow"), None), P(("blk", "narrow"), None), P("blk", None))
    return jax.shard_map(
        functools.partial(body, mesh.shape["blk"], mesh.shape["narrow"]),
        mesh=mesh,
        in_specs=placed,
        out_specs=(P(("blk", "narrow"), None), P(("blk", "narrow"), None)),
        check_vma=False,
    )
```

```python
import functools

import jax
import jax.numpy as jnp
from jax import lax
from jax.experimental import pallas as pl
from jax.experimental.pallas import tpu as pltpu
from jax.sharding import PartitionSpec as P

MESH = pl.DeviceIdType.MESH
VMEM = pltpu.VMEM
DMA = pltpu.SemaphoreType.DMA
HALVES = 2
CORES = 2


def flip(chip, distance):
    bit = 1
    while bit <= distance:
        if distance & bit:
            chip = chip + bit * (1 - 2 * ((chip // bit) % 2))
        bit *= 2
    return chip


def low(d):
    return d & -d


def high(d):
    return 1 << (d.bit_length() - 1)


def ones(d):
    return bin(d).count("1")


def bits_of(chips):
    return [1 << i for i in range(chips.bit_length() - 1)]


def toward(d, half):
    return low(d) if half == 0 else high(d)


def children(d, half, bits):
    return [b for b in bits if d == 0 or (b < low(d) if half == 0 else b > high(d))]


def pieces_of(chips):
    return [(d, h) for d in range(chips) for h in range(HALVES)]


def nt_dot(a, b):
    return lax.dot_general(a, b, (((1,), (1,)), ((), ())), preferred_element_type=jnp.float32)


def gather_kernel(
    chips, codes, signals, atoms, full, misfit, held, target, total,
    load_sem, target_sem, atom_sem, net_send, net_recv, core_send, core_recv,
):
    bits = bits_of(chips)
    me = lax.axis_index("blk")
    chip, core = me // CORES, me % CORES
    other = CORES * chip + 1 - core
    width = full.shape[2]

    def owner(d, c):
        return CORES * flip(chip, d) + c

    order = sorted(
        pieces_of(chips),
        key=lambda p: (ones(p[0]), -len(children(p[0], p[1], bits)), p[0]),
    )
    uses = [(d, h, c) for d, h in order for c in range(CORES)]

    def atom_copy(h):
        return pltpu.make_async_copy(
            atoms.at[:, pl.ds(h * width, width)], full.at[me * HALVES + h], atom_sem.at[h]
        )

    def block(d, h, c):
        return owner(d, core if c == 0 else 1 - core) * HALVES + h

    def load(slot):
        d, h, c = uses[slot]
        start = pl.multiple_of(block(d, h, c) * width, width)
        return pltpu.make_async_copy(
            codes.at[:, pl.ds(start, width)], held.at[slot], load_sem.at[slot]
        )

    for h in range(HALVES):
        atom_copy(h).start()
    partners = [other] + [CORES * flip(chip, b) + core for b in bits]
    barrier = pltpu.get_barrier_semaphore()
    for partner in partners:
        pl.semaphore_signal(barrier, inc=1, device_id={"blk": partner}, device_id_type=MESH)
    for slot in range(len(uses)):
        load(slot).start()

    target_copy = pltpu.make_async_copy(signals, target, target_sem)
    target_copy.start()

    sends = []

    def net(d, h, b):
        place = full.at[block(d, h, 0)]
        copy = pltpu.make_async_remote_copy(
            place, place, net_send.at[len(sends)], net_recv.at[(d ^ b) * HALVES + h],
            device_id={"blk": CORES * flip(chip, b) + core}, device_id_type=MESH,
        )
        copy.start()
        sends.append(copy)

    def across(d, h, c):
        place = full.at[block(d, h, c)]
        index = d * HALVES + h
        return pltpu.make_async_remote_copy(
            place, place, core_send.at[index], core_recv.at[index],
            device_id={"blk": other}, device_id_type=MESH,
        )

    def arrived(d, h):
        place = full.at[block(d, h, 0)]
        pltpu.make_async_remote_copy(
            place, place, net_send.at[0], net_recv.at[d * HALVES + h],
            device_id={"blk": other}, device_id_type=MESH,
        ).wait_recv()

    def use(d, h, c):
        slot = uses.index((d, h, c))
        load(slot).wait()
        total[...] += nt_dot(held[slot], full[block(d, h, c)])

    for h in range(HALVES):
        atom_copy(h).wait()
    pl.semaphore_wait(barrier, len(partners))
    for step in range(HALVES):
        for i, b in enumerate(bits):
            h = 1 - step if i == 0 else step
            net(0, h, b)
        across(0, step, 0).start()
    total[...] = jnp.zeros_like(total)
    waiting = []
    for d, h in order:
        if d:
            arrived(d, h)
            for b in children(d, h, bits):
                net(d, h, b)
            across(d, h, 0).start()
        use(d, h, 0)
        waiting.append((d, h))
        if len(waiting) > 1:
            e, k = waiting.pop(0)
            across(e, k, 1).wait_recv()
            use(e, k, 1)
    for e, k in waiting:
        across(e, k, 1).wait_recv()
        use(e, k, 1)
    target_copy.wait()
    rounded = (total[...] - target[...].astype(jnp.float32)).astype(jnp.bfloat16)
    misfit[...] = (rounded.astype(jnp.float32) * -4.0).astype(jnp.bfloat16)
    for copy in sends:
        copy.wait_send()
    for d, h in order:
        across(d, h, 0).wait_send()


def update_kernel(together, codes, signals, full, misfit, fresh, made, misfit_two, total, store_sem):
    blocks, _, width = full.shape

    def store(i):
        start = pl.multiple_of(i * width, width)
        return pltpu.make_async_copy(
            made.at[i], fresh.at[:, pl.ds(start, width)], store_sem.at[i]
        )

    total[...] = jnp.zeros_like(total)

    @pl.loop(0, blocks // together)
    def _(step):
        for j in range(together):
            i = step * together + j
            start = pl.multiple_of(i * width, width)
            change = jnp.dot(misfit[...], full[i], preferred_element_type=jnp.float32)
            moved = codes[:, pl.ds(start, width)].astype(jnp.float32) + change
            made[i] = (moved - jnp.clip(moved, -0.5, 0.5)).astype(jnp.bfloat16)
            store(i).start()
        for j in range(together):
            i = step * together + j
            total[...] += nt_dot(made[i], full[i])

    left = total[...] - signals[...].astype(jnp.float32)
    misfit_two[...] = left.T.astype(jnp.bfloat16)
    for i in range(blocks):
        store(i).wait()


def slices_of(features):
    unit = features // 12
    ranges, start = [], 0
    for size in (2 * unit, 2 * unit, unit, unit):
        ranges.append([(start, size), (start + size, size)])
        start += 2 * size
    return ranges


def gaps_of(chips):
    bits = bits_of(chips)
    return [
        (d, b) for d in range(chips) for b in bits
        if any(b in children(d, t, bits) for t in range(HALVES))
    ]


def gradient_kernel(
    chips, line, scale, made, misfit, grad,
    core_out, core_in, mine, net_out, net_in, own, z_out, z_in,
    core_send, core_recv, net_send, net_recv, z_send, z_recv,
):
    bits = bits_of(chips)
    gaps = gaps_of(chips)
    slices = slices_of(grad.shape[0])
    me = lax.axis_index("blk")
    z = lax.axis_index("narrow")
    chip, core = me // CORES, me % CORES
    other = CORES * chip + 1 - core
    width = made.shape[2]
    part = grad.shape[1]

    barrier = pltpu.get_barrier_semaphore()
    partners = [other] + [CORES * flip(chip, b) + core for b in bits]
    for partner in partners:
        pl.semaphore_signal(barrier, inc=1, device_id={"blk": partner}, device_id_type=MESH)
    beside = [(z + 1) % line, (z + line - 1) % line] if line > 1 else []
    for partner in beside:
        pl.semaphore_signal(barrier, inc=1, device_id={"narrow": partner}, device_id_type=MESH)

    def term(d, h, c):
        owner = CORES * flip(chip, d) + (core if c == 0 else 1 - core)
        return jnp.dot(misfit[...], made[owner * HALVES + h], preferred_element_type=jnp.float32)

    def across(d, h):
        i = d * HALVES + h
        return pltpu.make_async_remote_copy(
            core_out.at[i], core_in.at[i], core_send.at[i], core_recv.at[i],
            device_id={"blk": other}, device_id_type=MESH,
        )

    def hand_over(d):
        for h in range(HALVES):
            core_out[d * HALVES + h] = term(d, h, 1).astype(jnp.bfloat16)

    def sum_cores(d):
        for h in range(HALVES):
            value = term(d, h, 0)
            across(d, h).wait_recv()
            mine[d, :, h * width:(h + 1) * width] = value + core_in[d * HALVES + h].astype(jnp.float32)

    def net(d, k, t):
        b = toward(d, t)
        start, size = slices[k][t]
        gap = gaps.index((d ^ b, b))
        rows = pl.ds(start, size)
        return pltpu.make_async_remote_copy(
            net_out.at[d - 1, rows], net_in.at[gap, rows],
            net_send.at[d - 1, k, t], net_recv.at[gap, k, t],
            device_id={"blk": CORES * flip(chip, b) + core}, device_id_type=MESH,
        )

    def summed(d, k, t):
        start, size = slices[k][t]
        value = mine[d, start:start + size]
        for b in children(d, t, bits):
            gap = gaps.index((d, b))
            rows = pl.ds(start, size)
            pltpu.make_async_remote_copy(
                net_out.at[0, rows], net_in.at[gap, rows],
                net_send.at[0, k, t], net_recv.at[gap, k, t],
                device_id={"blk": other}, device_id_type=MESH,
            ).wait_recv()
            value += net_in[gap, start:start + size].astype(jnp.float32)
        return value

    def pass_on(d, k, t):
        start, size = slices[k][t]
        net_out[d - 1, start:start + size] = summed(d, k, t).astype(jnp.bfloat16)
        net(d, k, t).start()

    away = sorted(((d, t) for d in range(1, chips) for t in range(HALVES)), key=lambda p: -ones(p[0]))
    firsts = [p for p in away if not children(*p, bits)]
    relays = [p for p in away if children(*p, bits)]

    def arrive(k):
        for t in range(HALVES):
            start, size = slices[k][t]
            value = summed(0, k, t)
            for j in range(line):
                own[j, start:start + size] = value[:, j * part:(j + 1) * part]

    def span(k):
        start = slices[k][0][0]
        return start, sum(size for _, size in slices[k])

    def z_copy(k, side, t):
        rows = pl.ds(*span(k))
        return pltpu.make_async_remote_copy(
            z_out.at[side, t, rows], z_in.at[side, t - 1, rows],
            z_send.at[side, t, k], z_recv.at[side, t - 1, k],
            device_id={"narrow": z + 1 if side == 0 else z - 1}, device_id_type=MESH,
        )

    def z_arrived(k, side, t):
        rows = pl.ds(*span(k))
        pltpu.make_async_remote_copy(
            z_out.at[side, 0, rows], z_in.at[side, t, rows],
            z_send.at[side, 0, k], z_recv.at[side, t, k],
            device_id={"narrow": z - 1 if side == 0 else z + 1}, device_id_type=MESH,
        ).wait_recv()

    def has_behind(side):
        return z >= 1 if side == 0 else z <= line - 2

    def in_line(side, t):
        return z + t < line if side == 0 else z - t >= 0

    def z_step(k, t):
        start, size = span(k)
        rows = pl.ds(start, size)
        for side in range(2):
            @pl.when(in_line(side, t))
            def _():
                value = own[z + t if side == 0 else z - t, rows]

                @pl.when(has_behind(side))
                def _():
                    z_arrived(k, side, t)
                    z_out[side, t, rows] = (
                        value + z_in[side, t, rows].astype(jnp.float32)
                    ).astype(jnp.bfloat16)

                @pl.when(jnp.logical_not(has_behind(side)))
                def _():
                    z_out[side, t, rows] = value.astype(jnp.bfloat16)

                z_copy(k, side, t).start()

    def z_finish(k):
        rows = pl.ds(*span(k))
        grad[rows] = own[z, rows] * scale
        for side in range(2):
            @pl.when(has_behind(side))
            def _():
                z_arrived(k, side, 0)
                grad[rows] += z_in[side, 0, rows].astype(jnp.float32) * scale

    order = sorted(range(chips), key=lambda d: (-ones(d), d))
    hand_over(order[0])
    pl.semaphore_wait(barrier, len(partners) + len(beside))
    for h in range(HALVES):
        across(order[0], h).start()
    for i, d in enumerate(order):
        if i + 1 < chips:
            hand_over(order[i + 1])
            for h in range(HALVES):
                across(order[i + 1], h).start()
        sum_cores(d)
        for e, t in firsts:
            if e == d:
                pass_on(d, 0, t)
    count = len(slices)
    for k in range(1, min(2, count)):
        for d, t in firsts:
            pass_on(d, k, t)
    for now in range(count + line):
        if now < count:
            for d, t in relays:
                pass_on(d, now, t)
        if now + 2 < count:
            for d, t in firsts:
                pass_on(d, now + 2, t)
        if 1 <= now <= count:
            arrive(now - 1)
        for k in range(count):
            t = line - 1 - (now - 1 - k)
            if 1 <= t <= line - 1:
                z_step(k, t)
            elif t == 0:
                z_finish(k)

    for k in range(count):
        for d, t in away:
            net(d, k, t).wait_send()
        for t in range(1, line):
            for side in range(2):
                @pl.when(in_line(side, t))
                def _():
                    z_copy(k, side, t).wait_send()
    for d in range(chips):
        for h in range(HALVES):
            across(d, h).wait_send()


def in_hbm(array):
    return pltpu.with_memory_space_constraint(array, pltpu.HBM)


def body(blk, line, codes, signals, dictionary):
    rows, count = codes.shape
    atoms, features = dictionary.shape
    chips = blk // CORES
    width = atoms // HALVES
    blocks = blk * HALVES
    pieces = chips * HALVES
    part = atoms // line
    bf16, f32 = jnp.bfloat16, jnp.float32
    hbm_spec = pl.BlockSpec(memory_space=pltpu.HBM)
    vmem_spec = pl.BlockSpec(memory_space=VMEM)
    flops = 2 * rows * count * features
    size = 2 * rows * count

    full, misfit = pl.pallas_call(
        functools.partial(gather_kernel, chips),
        out_shape=(
            jax.ShapeDtypeStruct((blocks, features, width), bf16),
            jax.ShapeDtypeStruct((rows, features), bf16),
        ),
        in_specs=[hbm_spec] * 3,
        out_specs=(vmem_spec, vmem_spec),
        scratch_shapes=[
            VMEM((blocks, rows, width), bf16),
            VMEM((rows, features), bf16),
            VMEM((rows, features), f32),
            DMA((blocks,)), DMA, DMA((HALVES,)),
            DMA((HALVES * max(chips - 1, 1),)), DMA((pieces,)),
            DMA((pieces,)), DMA((pieces,)),
        ],
        compiler_params=pltpu.CompilerParams(
            collective_id=0, has_side_effects=True, vmem_limit_bytes=32 * 2**20
        ),
        cost_estimate=pl.CostEstimate(flops=flops, bytes_accessed=2 * size, transcendentals=0),
        name="gather_atoms",
    )(in_hbm(codes), in_hbm(signals), in_hbm(dictionary.T))

    fresh, made, misfit_two = pl.pallas_call(
        functools.partial(update_kernel, 4),
        out_shape=(
            jax.ShapeDtypeStruct((rows, count), bf16),
            jax.ShapeDtypeStruct((blocks, rows, width), bf16),
            jax.ShapeDtypeStruct((features, rows), bf16),
        ),
        in_specs=[vmem_spec] * 4,
        out_specs=(hbm_spec, vmem_spec, vmem_spec),
        scratch_shapes=[
            VMEM((rows, features), f32),
            DMA((blocks,)),
        ],
        compiler_params=pltpu.CompilerParams(vmem_limit_bytes=24 * 2**20),
        cost_estimate=pl.CostEstimate(flops=2 * flops, bytes_accessed=3 * size, transcendentals=0),
        name="update_codes",
    )(codes, signals, full, misfit)

    gaps = max(len(gaps_of(chips)), 1)
    far = max(chips - 1, 1)
    count_of = len(slices_of(features))
    grad = pl.pallas_call(
        functools.partial(gradient_kernel, chips, line, float(rows * blk * line) ** -0.5),
        out_shape=jax.ShapeDtypeStruct((features, part), f32),
        in_specs=[vmem_spec] * 2,
        out_specs=vmem_spec,
        scratch_shapes=[
            VMEM((pieces, features, width), bf16),
            VMEM((pieces, features, width), bf16),
            VMEM((chips, features, atoms), f32),
            VMEM((far, features, atoms), bf16),
            VMEM((gaps, features, atoms), bf16),
            VMEM((line, features, part), f32),
            VMEM((2, line, features, part), bf16),
            VMEM((2, line, features, part), bf16),
            DMA((pieces,)), DMA((pieces,)),
            DMA((far, count_of, HALVES)), DMA((gaps, count_of, HALVES)),
            DMA((2, line, count_of)), DMA((2, line, count_of)),
        ],
        compiler_params=pltpu.CompilerParams(
            collective_id=1, has_side_effects=True, vmem_limit_bytes=32 * 2**20
        ),
        cost_estimate=pl.CostEstimate(flops=flops, bytes_accessed=2 * size, transcendentals=0),
        name="dictionary_gradient",
    )(made, misfit_two)
    return fresh, grad.T


def solution(mesh):
    placed = (P(("blk", "narrow"), None), P(("blk", "narrow"), None), P("blk", None))
    return jax.shard_map(
        functools.partial(body, mesh.shape["blk"], mesh.shape["narrow"]),
        mesh=mesh,
        in_specs=placed,
        out_specs=(P(("blk", "narrow"), None), P(("blk", "narrow"), None)),
        check_vma=False,
    )
```

```python
import functools

import jax
import jax.numpy as jnp
from jax import lax
from jax.experimental import pallas as pl
from jax.experimental.pallas import tpu as pltpu
from jax.sharding import PartitionSpec as P

MESH = pl.DeviceIdType.MESH
VMEM = pltpu.VMEM
DMA = pltpu.SemaphoreType.DMA
HALVES = 2
CORES = 2


def flip(chip, distance):
    bit = 1
    while bit <= distance:
        if distance & bit:
            chip = chip + bit * (1 - 2 * ((chip // bit) % 2))
        bit *= 2
    return chip


def low(d):
    return d & -d


def high(d):
    return 1 << (d.bit_length() - 1)


def ones(d):
    return bin(d).count("1")


def bits_of(chips):
    return [1 << i for i in range(chips.bit_length() - 1)]


def toward(d, half):
    return low(d) if half == 0 else high(d)


def children(d, half, bits):
    return [b for b in bits if d == 0 or (b < low(d) if half == 0 else b > high(d))]


def pieces_of(chips):
    return [(d, h) for d in range(chips) for h in range(HALVES)]


def nt_dot(a, b):
    return lax.dot_general(a, b, (((1,), (1,)), ((), ())), preferred_element_type=jnp.float32)


def gather_kernel(
    chips, codes, signals, atoms, full, misfit, held, target, total,
    load_sem, target_sem, atom_sem, net_send, net_recv, core_send, core_recv,
):
    bits = bits_of(chips)
    me = lax.axis_index("blk")
    chip, core = me // CORES, me % CORES
    other = CORES * chip + 1 - core
    width = full.shape[2]

    def owner(d, c):
        return CORES * flip(chip, d) + c

    order = sorted(
        pieces_of(chips),
        key=lambda p: (ones(p[0]), -len(children(p[0], p[1], bits)), p[0]),
    )
    uses = [(d, h, c) for d, h in order for c in range(CORES)]

    def atom_copy(h):
        return pltpu.make_async_copy(
            atoms.at[:, pl.ds(h * width, width)], full.at[me * HALVES + h], atom_sem.at[h]
        )

    def block(d, h, c):
        return owner(d, core if c == 0 else 1 - core) * HALVES + h

    def load(slot):
        d, h, c = uses[slot]
        start = pl.multiple_of(block(d, h, c) * width, width)
        return pltpu.make_async_copy(
            codes.at[:, pl.ds(start, width)], held.at[slot], load_sem.at[slot]
        )

    for h in range(HALVES):
        atom_copy(h).start()
    partners = [other] + [CORES * flip(chip, b) + core for b in bits]
    barrier = pltpu.get_barrier_semaphore()
    for partner in partners:
        pl.semaphore_signal(barrier, inc=1, device_id={"blk": partner}, device_id_type=MESH)
    for slot in range(len(uses)):
        load(slot).start()

    target_copy = pltpu.make_async_copy(signals, target, target_sem)
    target_copy.start()

    sends = []

    def net(d, h, b):
        place = full.at[block(d, h, 0)]
        copy = pltpu.make_async_remote_copy(
            place, place, net_send.at[len(sends)], net_recv.at[(d ^ b) * HALVES + h],
            device_id={"blk": CORES * flip(chip, b) + core}, device_id_type=MESH,
        )
        copy.start()
        sends.append(copy)

    def across(d, h, c):
        place = full.at[block(d, h, c)]
        index = d * HALVES + h
        return pltpu.make_async_remote_copy(
            place, place, core_send.at[index], core_recv.at[index],
            device_id={"blk": other}, device_id_type=MESH,
        )

    def arrived(d, h):
        place = full.at[block(d, h, 0)]
        pltpu.make_async_remote_copy(
            place, place, net_send.at[0], net_recv.at[d * HALVES + h],
            device_id={"blk": other}, device_id_type=MESH,
        ).wait_recv()

    def use(d, h, c):
        slot = uses.index((d, h, c))
        load(slot).wait()
        total[...] += nt_dot(held[slot], full[block(d, h, c)])

    for h in range(HALVES):
        atom_copy(h).wait()
    pl.semaphore_wait(barrier, len(partners))
    for step in range(HALVES):
        for i, b in enumerate(bits):
            h = 1 - step if i == 0 else step
            net(0, h, b)
        across(0, step, 0).start()
    total[...] = jnp.zeros_like(total)
    waiting = []
    for d, h in order:
        if d:
            arrived(d, h)
            for b in children(d, h, bits):
                net(d, h, b)
            across(d, h, 0).start()
        use(d, h, 0)
        waiting.append((d, h))
        if len(waiting) > 1:
            e, k = waiting.pop(0)
            across(e, k, 1).wait_recv()
            use(e, k, 1)
    for e, k in waiting:
        across(e, k, 1).wait_recv()
        use(e, k, 1)
    target_copy.wait()
    rounded = (total[...] - target[...].astype(jnp.float32)).astype(jnp.bfloat16)
    misfit[...] = (rounded.astype(jnp.float32) * -4.0).astype(jnp.bfloat16)
    for copy in sends:
        copy.wait_send()
    for d, h in order:
        across(d, h, 0).wait_send()


def update_kernel(together, codes, signals, full, misfit, fresh, made, misfit_two, total, store_sem):
    blocks, _, width = full.shape

    def store(i):
        start = pl.multiple_of(i * width, width)
        return pltpu.make_async_copy(
            made.at[i], fresh.at[:, pl.ds(start, width)], store_sem.at[i]
        )

    total[...] = jnp.zeros_like(total)

    @pl.loop(0, blocks // together)
    def _(step):
        for j in range(together):
            i = step * together + j
            start = pl.multiple_of(i * width, width)
            change = jnp.dot(misfit[...], full[i], preferred_element_type=jnp.float32)
            moved = codes[:, pl.ds(start, width)].astype(jnp.float32) + change
            made[i] = (moved - jnp.clip(moved, -0.5, 0.5)).astype(jnp.bfloat16)
            store(i).start()
        for j in range(together):
            i = step * together + j
            total[...] += nt_dot(made[i], full[i])

    left = total[...] - signals[...].astype(jnp.float32)
    misfit_two[...] = left.T.astype(jnp.bfloat16)
    for i in range(blocks):
        store(i).wait()


def slices_of(features):
    unit = features // 12
    ranges, start = [], 0
    for size in (unit, 2 * unit, 2 * unit, unit):
        ranges.append([(start, size), (start + size, size)])
        start += 2 * size
    return ranges


def gaps_of(chips):
    bits = bits_of(chips)
    return [
        (d, b) for d in range(chips) for b in bits
        if any(b in children(d, t, bits) for t in range(HALVES))
    ]


def gradient_kernel(
    chips, line, scale, made, misfit, grad,
    core_out, core_in, mine, net_out, net_in, own, z_out, z_in,
    core_send, core_recv, net_send, net_recv, z_send, z_recv,
):
    bits = bits_of(chips)
    gaps = gaps_of(chips)
    slices = slices_of(grad.shape[0])
    me = lax.axis_index("blk")
    z = lax.axis_index("narrow")
    chip, core = me // CORES, me % CORES
    other = CORES * chip + 1 - core
    width = made.shape[2]
    part = grad.shape[1]

    barrier = pltpu.get_barrier_semaphore()
    partners = [other] + [CORES * flip(chip, b) + core for b in bits]
    for partner in partners:
        pl.semaphore_signal(barrier, inc=1, device_id={"blk": partner}, device_id_type=MESH)
    beside = [(z + 1) % line, (z + line - 1) % line] if line > 1 else []
    for partner in beside:
        pl.semaphore_signal(barrier, inc=1, device_id={"narrow": partner}, device_id_type=MESH)

    def term(d, h, c):
        owner = CORES * flip(chip, d) + (core if c == 0 else 1 - core)
        return jnp.dot(misfit[...], made[owner * HALVES + h], preferred_element_type=jnp.float32)

    def span(k):
        start = slices[k][0][0]
        return start, sum(size for _, size in slices[k])

    def across(d, k):
        rows = pl.ds(*span(k))
        return pltpu.make_async_remote_copy(
            core_out.at[d, rows], core_in.at[d, rows], core_send.at[d, k], core_recv.at[d, k],
            device_id={"blk": other}, device_id_type=MESH,
        )

    def compute(into, d, c):
        for h in range(HALVES):
            into[d, :, h * width:(h + 1) * width] = term(d, h, c).astype(into.dtype)

    def net(d, k, t):
        b = toward(d, t)
        start, size = slices[k][t]
        gap = gaps.index((d ^ b, b))
        rows = pl.ds(start, size)
        return pltpu.make_async_remote_copy(
            net_out.at[d - 1, rows], net_in.at[gap, rows],
            net_send.at[d - 1, k, t], net_recv.at[gap, k, t],
            device_id={"blk": CORES * flip(chip, b) + core}, device_id_type=MESH,
        )

    def summed(d, k, t):
        start, size = slices[k][t]
        value = mine[d, start:start + size] + core_in[d, start:start + size].astype(jnp.float32)
        for b in children(d, t, bits):
            gap = gaps.index((d, b))
            rows = pl.ds(start, size)
            pltpu.make_async_remote_copy(
                net_out.at[0, rows], net_in.at[gap, rows],
                net_send.at[0, k, t], net_recv.at[gap, k, t],
                device_id={"blk": other}, device_id_type=MESH,
            ).wait_recv()
            value += net_in[gap, start:start + size].astype(jnp.float32)
        return value

    def pass_on(d, k, t):
        start, size = slices[k][t]
        net_out[d - 1, start:start + size] = summed(d, k, t).astype(jnp.bfloat16)
        net(d, k, t).start()

    away = sorted(((d, t) for d in range(1, chips) for t in range(HALVES)), key=lambda p: -ones(p[0]))
    firsts = [p for p in away if not children(*p, bits)]
    relays = [p for p in away if children(*p, bits)]

    def arrive(k):
        for t in range(HALVES):
            start, size = slices[k][t]
            value = summed(0, k, t)
            for j in range(line):
                own[j, start:start + size] = value[:, j * part:(j + 1) * part]

    def z_copy(k, side, t):
        rows = pl.ds(*span(k))
        return pltpu.make_async_remote_copy(
            z_out.at[side, t, rows], z_in.at[side, t - 1, rows],
            z_send.at[side, t, k], z_recv.at[side, t - 1, k],
            device_id={"narrow": z + 1 if side == 0 else z - 1}, device_id_type=MESH,
        )

    def z_arrived(k, side, t):
        rows = pl.ds(*span(k))
        pltpu.make_async_remote_copy(
            z_out.at[side, 0, rows], z_in.at[side, t, rows],
            z_send.at[side, 0, k], z_recv.at[side, t, k],
            device_id={"narrow": z - 1 if side == 0 else z + 1}, device_id_type=MESH,
        ).wait_recv()

    def has_behind(side):
        return z >= 1 if side == 0 else z <= line - 2

    def in_line(side, t):
        return z + t < line if side == 0 else z - t >= 0

    def z_step(k, t):
        start, size = span(k)
        rows = pl.ds(start, size)
        for side in range(2):
            @pl.when(in_line(side, t))
            def _():
                value = own[z + t if side == 0 else z - t, rows]

                @pl.when(has_behind(side))
                def _():
                    z_arrived(k, side, t)
                    z_out[side, t, rows] = (
                        value + z_in[side, t, rows].astype(jnp.float32)
                    ).astype(jnp.bfloat16)

                @pl.when(jnp.logical_not(has_behind(side)))
                def _():
                    z_out[side, t, rows] = value.astype(jnp.bfloat16)

                z_copy(k, side, t).start()

    def z_finish(k):
        rows = pl.ds(*span(k))
        grad[rows] = own[z, rows] * scale
        for side in range(2):
            @pl.when(has_behind(side))
            def _():
                z_arrived(k, side, 0)
                grad[rows] += z_in[side, 0, rows].astype(jnp.float32) * scale

    order = sorted(range(chips), key=lambda d: (-ones(d), d))
    count = len(slices)
    for i, d in enumerate(order):
        compute(core_out, d, 1)
        if i == 0:
            pl.semaphore_wait(barrier, len(partners) + len(beside))
        across(d, 0).start()
    for d in order:
        across(d, 1).start()

    def begin(d, k):
        across(d, k).wait_recv()
        for e, t in firsts:
            if e == d:
                pass_on(d, k, t)

    for d in order:
        compute(mine, d, 0)
        begin(d, 0)
    for now in range(count + line):
        if now + 2 < count:
            for d in order:
                across(d, now + 2).start()
        if now < count:
            for d, t in relays:
                pass_on(d, now, t)
        if now + 1 < count:
            for d in order:
                begin(d, now + 1)
        if 1 <= now <= count:
            arrive(now - 1)
        for k in range(count):
            t = line - 1 - (now - 1 - k)
            if 1 <= t <= line - 1:
                z_step(k, t)
            elif t == 0:
                z_finish(k)

    for k in range(count):
        for d, t in away:
            net(d, k, t).wait_send()
        for t in range(1, line):
            for side in range(2):
                @pl.when(in_line(side, t))
                def _():
                    z_copy(k, side, t).wait_send()
    for k in range(count):
        for d in order:
            across(d, k).wait_send()


def in_hbm(array):
    return pltpu.with_memory_space_constraint(array, pltpu.HBM)


def body(blk, line, codes, signals, dictionary):
    rows, count = codes.shape
    atoms, features = dictionary.shape
    chips = blk // CORES
    width = atoms // HALVES
    blocks = blk * HALVES
    pieces = chips * HALVES
    part = atoms // line
    bf16, f32 = jnp.bfloat16, jnp.float32
    hbm_spec = pl.BlockSpec(memory_space=pltpu.HBM)
    vmem_spec = pl.BlockSpec(memory_space=VMEM)
    flops = 2 * rows * count * features
    size = 2 * rows * count

    full, misfit = pl.pallas_call(
        functools.partial(gather_kernel, chips),
        out_shape=(
            jax.ShapeDtypeStruct((blocks, features, width), bf16),
            jax.ShapeDtypeStruct((rows, features), bf16),
        ),
        in_specs=[hbm_spec] * 3,
        out_specs=(vmem_spec, vmem_spec),
        scratch_shapes=[
            VMEM((blocks, rows, width), bf16),
            VMEM((rows, features), bf16),
            VMEM((rows, features), f32),
            DMA((blocks,)), DMA, DMA((HALVES,)),
            DMA((HALVES * max(chips - 1, 1),)), DMA((pieces,)),
            DMA((pieces,)), DMA((pieces,)),
        ],
        compiler_params=pltpu.CompilerParams(
            collective_id=0, has_side_effects=True, vmem_limit_bytes=32 * 2**20
        ),
        cost_estimate=pl.CostEstimate(flops=flops, bytes_accessed=2 * size, transcendentals=0),
        name="gather_atoms",
    )(in_hbm(codes), in_hbm(signals), in_hbm(dictionary.T))

    fresh, made, misfit_two = pl.pallas_call(
        functools.partial(update_kernel, 4),
        out_shape=(
            jax.ShapeDtypeStruct((rows, count), bf16),
            jax.ShapeDtypeStruct((blocks, rows, width), bf16),
            jax.ShapeDtypeStruct((features, rows), bf16),
        ),
        in_specs=[vmem_spec] * 4,
        out_specs=(hbm_spec, vmem_spec, vmem_spec),
        scratch_shapes=[
            VMEM((rows, features), f32),
            DMA((blocks,)),
        ],
        compiler_params=pltpu.CompilerParams(vmem_limit_bytes=24 * 2**20),
        cost_estimate=pl.CostEstimate(flops=2 * flops, bytes_accessed=3 * size, transcendentals=0),
        name="update_codes",
    )(codes, signals, full, misfit)

    gaps = max(len(gaps_of(chips)), 1)
    far = max(chips - 1, 1)
    count_of = len(slices_of(features))
    grad = pl.pallas_call(
        functools.partial(gradient_kernel, chips, line, float(rows * blk * line) ** -0.5),
        out_shape=jax.ShapeDtypeStruct((features, part), f32),
        in_specs=[vmem_spec] * 2,
        out_specs=vmem_spec,
        scratch_shapes=[
            VMEM((chips, features, atoms), bf16),
            VMEM((chips, features, atoms), bf16),
            VMEM((chips, features, atoms), f32),
            VMEM((far, features, atoms), bf16),
            VMEM((gaps, features, atoms), bf16),
            VMEM((line, features, part), f32),
            VMEM((2, line, features, part), bf16),
            VMEM((2, line, features, part), bf16),
            DMA((chips, count_of)), DMA((chips, count_of)),
            DMA((far, count_of, HALVES)), DMA((gaps, count_of, HALVES)),
            DMA((2, line, count_of)), DMA((2, line, count_of)),
        ],
        compiler_params=pltpu.CompilerParams(
            collective_id=1, has_side_effects=True, vmem_limit_bytes=32 * 2**20
        ),
        cost_estimate=pl.CostEstimate(flops=flops, bytes_accessed=2 * size, transcendentals=0),
        name="dictionary_gradient",
    )(made, misfit_two)
    return fresh, grad.T


def solution(mesh):
    placed = (P(("blk", "narrow"), None), P(("blk", "narrow"), None), P("blk", None))
    return jax.shard_map(
        functools.partial(body, mesh.shape["blk"], mesh.shape["narrow"]),
        mesh=mesh,
        in_specs=placed,
        out_specs=(P(("blk", "narrow"), None), P(("blk", "narrow"), None)),
        check_vma=False,
    )
```

```python
import functools

import jax
import jax.numpy as jnp
from jax import lax
from jax.experimental import pallas as pl
from jax.experimental.pallas import tpu as pltpu
from jax.sharding import PartitionSpec as P

MESH = pl.DeviceIdType.MESH
VMEM = pltpu.VMEM
DMA = pltpu.SemaphoreType.DMA
HALVES = 2
CORES = 2


def flip(chip, distance):
    bit = 1
    while bit <= distance:
        if distance & bit:
            chip = chip + bit * (1 - 2 * ((chip // bit) % 2))
        bit *= 2
    return chip


def low(d):
    return d & -d


def high(d):
    return 1 << (d.bit_length() - 1)


def ones(d):
    return bin(d).count("1")


def bits_of(chips):
    return [1 << i for i in range(chips.bit_length() - 1)]


def toward(d, half):
    return low(d) if half == 0 else high(d)


def children(d, half, bits):
    return [b for b in bits if d == 0 or (b < low(d) if half == 0 else b > high(d))]


def pieces_of(chips):
    return [(d, h) for d in range(chips) for h in range(HALVES)]


def nt_dot(a, b):
    return lax.dot_general(a, b, (((1,), (1,)), ((), ())), preferred_element_type=jnp.float32)


def gather_kernel(
    chips, codes, signals, atoms, full, misfit, held, target, total,
    load_sem, target_sem, atom_sem, net_send, net_recv, core_send, core_recv,
):
    bits = bits_of(chips)
    me = lax.axis_index("blk")
    chip, core = me // CORES, me % CORES
    other = CORES * chip + 1 - core
    width = full.shape[2]

    def owner(d, c):
        return CORES * flip(chip, d) + c

    order = sorted(
        pieces_of(chips),
        key=lambda p: (ones(p[0]), -len(children(p[0], p[1], bits)), p[0]),
    )
    uses = [(d, h, c) for d, h in order for c in range(CORES)]

    def atom_copy(h):
        return pltpu.make_async_copy(
            atoms.at[:, pl.ds(h * width, width)], full.at[me * HALVES + h], atom_sem.at[h]
        )

    def block(d, h, c):
        return owner(d, core if c == 0 else 1 - core) * HALVES + h

    def load(slot):
        d, h, c = uses[slot]
        start = pl.multiple_of(block(d, h, c) * width, width)
        return pltpu.make_async_copy(
            codes.at[:, pl.ds(start, width)], held.at[slot], load_sem.at[slot]
        )

    for h in range(HALVES):
        atom_copy(h).start()
    partners = [other] + [CORES * flip(chip, b) + core for b in bits]
    barrier = pltpu.get_barrier_semaphore()
    for partner in partners:
        pl.semaphore_signal(barrier, inc=1, device_id={"blk": partner}, device_id_type=MESH)
    for slot in range(len(uses)):
        load(slot).start()

    target_copy = pltpu.make_async_copy(signals, target, target_sem)
    target_copy.start()

    sends = []

    def net(d, h, b):
        place = full.at[block(d, h, 0)]
        copy = pltpu.make_async_remote_copy(
            place, place, net_send.at[len(sends)], net_recv.at[(d ^ b) * HALVES + h],
            device_id={"blk": CORES * flip(chip, b) + core}, device_id_type=MESH,
        )
        copy.start()
        sends.append(copy)

    def across(d, h, c):
        place = full.at[block(d, h, c)]
        index = d * HALVES + h
        return pltpu.make_async_remote_copy(
            place, place, core_send.at[index], core_recv.at[index],
            device_id={"blk": other}, device_id_type=MESH,
        )

    def arrived(d, h):
        place = full.at[block(d, h, 0)]
        pltpu.make_async_remote_copy(
            place, place, net_send.at[0], net_recv.at[d * HALVES + h],
            device_id={"blk": other}, device_id_type=MESH,
        ).wait_recv()

    def use(d, h, c):
        slot = uses.index((d, h, c))
        load(slot).wait()
        total[...] += nt_dot(held[slot], full[block(d, h, c)])

    for h in range(HALVES):
        atom_copy(h).wait()
    pl.semaphore_wait(barrier, len(partners))
    for step in range(HALVES):
        for i, b in enumerate(bits):
            h = 1 - step if i == 0 else step
            net(0, h, b)
        across(0, step, 0).start()
    total[...] = jnp.zeros_like(total)
    waiting = []
    for d, h in order:
        if d:
            arrived(d, h)
            for b in children(d, h, bits):
                net(d, h, b)
            across(d, h, 0).start()
        use(d, h, 0)
        waiting.append((d, h))
        if len(waiting) > 1:
            e, k = waiting.pop(0)
            across(e, k, 1).wait_recv()
            use(e, k, 1)
    for e, k in waiting:
        across(e, k, 1).wait_recv()
        use(e, k, 1)
    target_copy.wait()
    rounded = (total[...] - target[...].astype(jnp.float32)).astype(jnp.bfloat16)
    misfit[...] = (rounded.astype(jnp.float32) * -4.0).astype(jnp.bfloat16)
    for copy in sends:
        copy.wait_send()
    for d, h in order:
        across(d, h, 0).wait_send()


def update_kernel(together, codes, signals, full, misfit, fresh, made, misfit_two, total, store_sem):
    blocks, _, width = full.shape

    def store(i):
        start = pl.multiple_of(i * width, width)
        return pltpu.make_async_copy(
            made.at[i], fresh.at[:, pl.ds(start, width)], store_sem.at[i]
        )

    total[...] = jnp.zeros_like(total)

    @pl.loop(0, blocks // together)
    def _(step):
        for j in range(together):
            i = step * together + j
            start = pl.multiple_of(i * width, width)
            change = jnp.dot(misfit[...], full[i], preferred_element_type=jnp.float32)
            moved = codes[:, pl.ds(start, width)].astype(jnp.float32) + change
            made[i] = (moved - jnp.clip(moved, -0.5, 0.5)).astype(jnp.bfloat16)
            store(i).start()
        for j in range(together):
            i = step * together + j
            total[...] += nt_dot(made[i], full[i])

    left = total[...] - signals[...].astype(jnp.float32)
    misfit_two[...] = left.T.astype(jnp.bfloat16)
    for i in range(blocks):
        store(i).wait()


def slices_of(features):
    unit = features // 12
    ranges, start = [], 0
    for size in (unit, 2 * unit, 2 * unit, unit):
        ranges.append([(start, size), (start + size, size)])
        start += 2 * size
    return ranges


def gaps_of(chips):
    bits = bits_of(chips)
    return [
        (d, b) for d in range(chips) for b in bits
        if any(b in children(d, t, bits) for t in range(HALVES))
    ]


def gradient_kernel(
    chips, line, scale, made, misfit, grad,
    core_out, core_in, mine, net_out, net_in, own, z_out, z_in,
    core_send, core_recv, net_send, net_recv, z_send, z_recv,
):
    bits = bits_of(chips)
    gaps = gaps_of(chips)
    slices = slices_of(grad.shape[0])
    me = lax.axis_index("blk")
    z = lax.axis_index("narrow")
    chip, core = me // CORES, me % CORES
    other = CORES * chip + 1 - core
    width = made.shape[2]
    part = grad.shape[1]

    barrier = pltpu.get_barrier_semaphore()
    partners = [other] + [CORES * flip(chip, b) + core for b in bits]
    for partner in partners:
        pl.semaphore_signal(barrier, inc=1, device_id={"blk": partner}, device_id_type=MESH)
    beside = [(z + t) % line for t in range(1, line)]
    for partner in beside:
        pl.semaphore_signal(barrier, inc=1, device_id={"narrow": partner}, device_id_type=MESH)

    def term(d, h, c):
        owner = CORES * flip(chip, d) + (core if c == 0 else 1 - core)
        return jnp.dot(misfit[...], made[owner * HALVES + h], preferred_element_type=jnp.float32)

    def span(k):
        start = slices[k][0][0]
        return start, sum(size for _, size in slices[k])

    def across(d, k):
        rows = pl.ds(*span(k))
        return pltpu.make_async_remote_copy(
            core_out.at[d, rows], core_in.at[d, rows], core_send.at[d, k], core_recv.at[d, k],
            device_id={"blk": other}, device_id_type=MESH,
        )

    def compute(into, d, c):
        for h in range(HALVES):
            into[d, :, h * width:(h + 1) * width] = term(d, h, c).astype(into.dtype)

    def net(d, k, t):
        b = toward(d, t)
        start, size = slices[k][t]
        gap = gaps.index((d ^ b, b))
        rows = pl.ds(start, size)
        return pltpu.make_async_remote_copy(
            net_out.at[d - 1, rows], net_in.at[gap, rows],
            net_send.at[d - 1, k, t], net_recv.at[gap, k, t],
            device_id={"blk": CORES * flip(chip, b) + core}, device_id_type=MESH,
        )

    def summed(d, k, t):
        start, size = slices[k][t]
        value = mine[d, start:start + size] + core_in[d, start:start + size].astype(jnp.float32)
        for b in children(d, t, bits):
            gap = gaps.index((d, b))
            rows = pl.ds(start, size)
            pltpu.make_async_remote_copy(
                net_out.at[0, rows], net_in.at[gap, rows],
                net_send.at[0, k, t], net_recv.at[gap, k, t],
                device_id={"blk": other}, device_id_type=MESH,
            ).wait_recv()
            value += net_in[gap, start:start + size].astype(jnp.float32)
        return value

    def pass_on(d, k, t):
        start, size = slices[k][t]
        net_out[d - 1, start:start + size] = summed(d, k, t).astype(jnp.bfloat16)
        net(d, k, t).start()

    away = sorted(((d, t) for d in range(1, chips) for t in range(HALVES)), key=lambda p: -ones(p[0]))
    firsts = [p for p in away if not children(*p, bits)]
    relays = [p for p in away if children(*p, bits)]

    def arrive(k):
        for t in range(HALVES):
            start, size = slices[k][t]
            value = summed(0, k, t)
            for j in range(line):
                own[j, start:start + size] = value[:, j * part:(j + 1) * part]

    def z_copy(k, t):
        rows = pl.ds(*span(k))
        return pltpu.make_async_remote_copy(
            z_out.at[t - 1, rows], z_in.at[t - 1, rows], z_send.at[t - 1, k], z_recv.at[t - 1, k],
            device_id={"narrow": (z + t) % line}, device_id_type=MESH,
        )

    def spread(k):
        rows = pl.ds(*span(k))
        for t in range(line - 1, 0, -1):
            z_out[t - 1, rows] = own[(z + t) % line, rows].astype(jnp.bfloat16)
            z_copy(k, t).start()

    def finish(k):
        rows = pl.ds(*span(k))
        value = own[z, rows]
        for t in range(1, line):
            z_copy(k, t).wait_recv()
            value += z_in[t - 1, rows].astype(jnp.float32)
        grad[rows] = value * scale

    order = sorted(range(chips), key=lambda d: (-ones(d), d))
    count = len(slices)
    for i, d in enumerate(order):
        compute(core_out, d, 1)
        if i == 0:
            pl.semaphore_wait(barrier, len(partners) + len(beside))
        across(d, 0).start()
    for d in order:
        across(d, 1).start()

    def begin(d, k):
        across(d, k).wait_recv()
        for e, t in firsts:
            if e == d:
                pass_on(d, k, t)

    for d in order:
        compute(mine, d, 0)
        begin(d, 0)
    for now in range(count + 3):
        if now + 2 < count:
            for d in order:
                across(d, now + 2).start()
        if now < count:
            for d, t in relays:
                pass_on(d, now, t)
        if now + 1 < count:
            for d in order:
                begin(d, now + 1)
        if 1 <= now <= count:
            arrive(now - 1)
            spread(now - 1)
        if now >= 3:
            finish(now - 3)

    for k in range(count):
        for d in order:
            across(d, k).wait_send()
        for d, t in away:
            net(d, k, t).wait_send()
        for t in range(1, line):
            z_copy(k, t).wait_send()


def in_hbm(array):
    return pltpu.with_memory_space_constraint(array, pltpu.HBM)


def body(blk, line, codes, signals, dictionary):
    rows, count = codes.shape
    atoms, features = dictionary.shape
    chips = blk // CORES
    width = atoms // HALVES
    blocks = blk * HALVES
    pieces = chips * HALVES
    part = atoms // line
    bf16, f32 = jnp.bfloat16, jnp.float32
    hbm_spec = pl.BlockSpec(memory_space=pltpu.HBM)
    vmem_spec = pl.BlockSpec(memory_space=VMEM)
    flops = 2 * rows * count * features
    size = 2 * rows * count

    full, misfit = pl.pallas_call(
        functools.partial(gather_kernel, chips),
        out_shape=(
            jax.ShapeDtypeStruct((blocks, features, width), bf16),
            jax.ShapeDtypeStruct((rows, features), bf16),
        ),
        in_specs=[hbm_spec] * 3,
        out_specs=(vmem_spec, vmem_spec),
        scratch_shapes=[
            VMEM((blocks, rows, width), bf16),
            VMEM((rows, features), bf16),
            VMEM((rows, features), f32),
            DMA((blocks,)), DMA, DMA((HALVES,)),
            DMA((HALVES * max(chips - 1, 1),)), DMA((pieces,)),
            DMA((pieces,)), DMA((pieces,)),
        ],
        compiler_params=pltpu.CompilerParams(
            collective_id=0, has_side_effects=True, vmem_limit_bytes=32 * 2**20
        ),
        cost_estimate=pl.CostEstimate(flops=flops, bytes_accessed=2 * size, transcendentals=0),
        name="gather_atoms",
    )(in_hbm(codes), in_hbm(signals), in_hbm(dictionary.T))

    fresh, made, misfit_two = pl.pallas_call(
        functools.partial(update_kernel, 4),
        out_shape=(
            jax.ShapeDtypeStruct((rows, count), bf16),
            jax.ShapeDtypeStruct((blocks, rows, width), bf16),
            jax.ShapeDtypeStruct((features, rows), bf16),
        ),
        in_specs=[vmem_spec] * 4,
        out_specs=(hbm_spec, vmem_spec, vmem_spec),
        scratch_shapes=[
            VMEM((rows, features), f32),
            DMA((blocks,)),
        ],
        compiler_params=pltpu.CompilerParams(vmem_limit_bytes=24 * 2**20),
        cost_estimate=pl.CostEstimate(flops=2 * flops, bytes_accessed=3 * size, transcendentals=0),
        name="update_codes",
    )(codes, signals, full, misfit)

    gaps = max(len(gaps_of(chips)), 1)
    far = max(chips - 1, 1)
    count_of = len(slices_of(features))
    grad = pl.pallas_call(
        functools.partial(gradient_kernel, chips, line, float(rows * blk * line) ** -0.5),
        out_shape=jax.ShapeDtypeStruct((features, part), f32),
        in_specs=[vmem_spec] * 2,
        out_specs=vmem_spec,
        scratch_shapes=[
            VMEM((chips, features, atoms), bf16),
            VMEM((chips, features, atoms), bf16),
            VMEM((chips, features, atoms), f32),
            VMEM((far, features, atoms), bf16),
            VMEM((gaps, features, atoms), bf16),
            VMEM((line, features, part), f32),
            VMEM((max(line - 1, 1), features, part), bf16),
            VMEM((max(line - 1, 1), features, part), bf16),
            DMA((chips, count_of)), DMA((chips, count_of)),
            DMA((far, count_of, HALVES)), DMA((gaps, count_of, HALVES)),
            DMA((max(line - 1, 1), count_of)), DMA((max(line - 1, 1), count_of)),
        ],
        compiler_params=pltpu.CompilerParams(
            collective_id=1, has_side_effects=True, vmem_limit_bytes=32 * 2**20
        ),
        cost_estimate=pl.CostEstimate(flops=flops, bytes_accessed=2 * size, transcendentals=0),
        name="dictionary_gradient",
    )(made, misfit_two)
    return fresh, grad.T


def solution(mesh):
    placed = (P(("blk", "narrow"), None), P(("blk", "narrow"), None), P("blk", None))
    return jax.shard_map(
        functools.partial(body, mesh.shape["blk"], mesh.shape["narrow"]),
        mesh=mesh,
        in_specs=placed,
        out_specs=(P(("blk", "narrow"), None), P(("blk", "narrow"), None)),
        check_vma=False,
    )
```

```python
import functools

import jax
import jax.numpy as jnp
from jax import lax
from jax.experimental import pallas as pl
from jax.experimental.pallas import tpu as pltpu
from jax.sharding import PartitionSpec as P

MESH = pl.DeviceIdType.MESH
VMEM = pltpu.VMEM
DMA = pltpu.SemaphoreType.DMA
TREES = 2
UNITS = 6
CORES = 2


def flip(chip, distance):
    bit = 1
    while bit <= distance:
        if distance & bit:
            chip = chip + bit * (1 - 2 * ((chip // bit) % 2))
        bit *= 2
    return chip


def low(d):
    return d & -d


def high(d):
    return 1 << (d.bit_length() - 1)


def ones(d):
    return bin(d).count("1")


def bits_of(chips):
    return [1 << i for i in range(chips.bit_length() - 1)]


def toward(d, half):
    return low(d) if half == 0 else high(d)


def children(d, half, bits):
    return [b for b in bits if d == 0 or (b < low(d) if half == 0 else b > high(d))]


def nt_dot(a, b):
    return lax.dot_general(a, b, (((1,), (1,)), ((), ())), preferred_element_type=jnp.float32)


def gather_kernel(
    chips, line, codes, signals, atoms, full, misfit, held, target, total,
    load_sem, target_sem, atom_sem, net_send, net_recv, pair_send, core_send, core_recv,
):
    bits = bits_of(chips)
    me = lax.axis_index("blk")
    z = lax.axis_index("narrow")
    odd = z % 2
    chip, core = me // CORES, me % CORES
    other = CORES * chip + 1 - core
    width = full.shape[2]
    paired = line % 2 == 0
    lead, rest, late = ([2, 3], [0, 1], [4, 5]) if paired else ([], list(range(UNITS)), [])

    def branches(d, u):
        return [] if u in late else children(d, u % TREES, bits)

    def block(d, u, c):
        unit = u
        if u in lead:
            unit = u + 2 * odd
        if u in late:
            unit = u - 2 * odd
        return (CORES * flip(chip, d) + (core if c == 0 else 1 - core)) * UNITS + unit

    def key(piece):
        return ones(piece[0]), -len(branches(*piece)), piece

    def sort(units, hops):
        return sorted([(d, u) for d in range(1, chips) if ones(d) in hops for u in units], key=key)

    near, distant = [1], range(2, chips)
    order = sort(lead, near) + sort(lead, distant) + sort(rest, near) + sort(late, near)
    order += sort(late, distant) + sort(rest, distant)
    own = [(0, u) for u in range(UNITS)]
    uses = [(d, u, c) for c in range(CORES) for d, u in own]
    uses += [(d, u, c) for d, u in order for c in range(CORES)]

    atom_copies = [
        pltpu.make_async_copy(
            atoms.at[:, pl.ds(u * width, width)], full.at[me * UNITS + u], atom_sem.at[u]
        )
        for u in range(UNITS)
    ]
    for copy in atom_copies:
        copy.start()
    partners = [{"blk": other}] + [{"blk": CORES * flip(chip, b) + core} for b in bits]
    if paired:
        partners.append({"narrow": z + 1 - 2 * odd})
    barrier = pltpu.get_barrier_semaphore()
    for partner in partners:
        pl.semaphore_signal(barrier, inc=1, device_id=partner, device_id_type=MESH)

    def load(slot):
        start = pl.multiple_of(block(*uses[slot]) * width, width)
        return pltpu.make_async_copy(
            codes.at[:, pl.ds(start, width)], held.at[slot], load_sem.at[slot]
        )

    for slot in range(len(uses)):
        load(slot).start()
    target_copy = pltpu.make_async_copy(signals, target, target_sem)
    target_copy.start()

    sends = []

    def net(d, u, b):
        place = full.at[block(d, u, 0)]
        copy = pltpu.make_async_remote_copy(
            place, place, net_send.at[len(sends)], net_recv.at[d ^ b, u],
            device_id={"blk": CORES * flip(chip, b) + core}, device_id_type=MESH,
        )
        copy.start()
        sends.append(copy)

    def pair(d, u):
        place = full.at[block(d, u, 0)]
        return pltpu.make_async_remote_copy(
            place, place, pair_send.at[d, u - lead[0]], net_recv.at[d, u + 2],
            device_id={"narrow": z + 1 - 2 * odd}, device_id_type=MESH,
        )

    def across(d, u, c):
        place = full.at[block(d, u, c)]
        return pltpu.make_async_remote_copy(
            place, place, core_send.at[d, u], core_recv.at[d, u],
            device_id={"blk": other}, device_id_type=MESH,
        )

    def arrived(d, u):
        place = full.at[block(d, u, 0)]
        pltpu.make_async_remote_copy(
            place, place, net_send.at[0], net_recv.at[d, u],
            device_id={"blk": other}, device_id_type=MESH,
        ).wait_recv()

    def use(d, u, c):
        slot = uses.index((d, u, c))
        load(slot).wait()
        total[...] += nt_dot(held[slot], full[block(d, u, c)])

    def send_own(units):
        for step in range(len(units)):
            for i, b in enumerate(bits):
                net(0, units[-1 - step] if i == 0 else units[step], b)

    for copy in atom_copies:
        copy.wait()
    pl.semaphore_wait(barrier, len(partners))
    send_own(lead or rest)
    for d, u in own:
        across(d, u, 0).start()
    total[...] = jnp.zeros_like(total)
    for d, u in own:
        use(d, u, 0)
    waiting = []
    relayed = 0
    for d, u in order:
        arrived(d, u)
        for b in branches(d, u):
            net(d, u, b)
        if u in lead:
            pair(d, u).start()
        across(d, u, 0).start()
        relayed += 1
        if lead and relayed == min(len(bits), len(order)):
            send_own(rest)
        if relayed == len(bits):
            for e, v in own:
                across(e, v, 1).wait_recv()
                use(e, v, 1)
        use(d, u, 0)
        waiting.append((d, u))
        if len(waiting) > 2:
            e, v = waiting.pop(0)
            across(e, v, 1).wait_recv()
            use(e, v, 1)
    for e, v in waiting:
        across(e, v, 1).wait_recv()
        use(e, v, 1)
    target_copy.wait()
    rounded = (total[...] - target[...].astype(jnp.float32)).astype(jnp.bfloat16)
    misfit[...] = (rounded.astype(jnp.float32) * -4.0).astype(jnp.bfloat16)
    for copy in sends:
        copy.wait_send()
    for d, u in own + order:
        across(d, u, 0).wait_send()
        if d and u in lead:
            pair(d, u).wait_send()


def update_kernel(together, codes, signals, full, misfit, fresh, made, misfit_two, total, store_sem):
    blocks, _, width = full.shape

    def store(i):
        start = pl.multiple_of(i * width, width)
        return pltpu.make_async_copy(
            made.at[i], fresh.at[:, pl.ds(start, width)], store_sem.at[i]
        )

    total[...] = jnp.zeros_like(total)

    @pl.loop(0, blocks // together)
    def _(step):
        for j in range(together):
            i = step * together + j
            start = pl.multiple_of(i * width, width)
            change = jnp.dot(misfit[...], full[i], preferred_element_type=jnp.float32)
            moved = codes[:, pl.ds(start, width)].astype(jnp.float32) + change
            made[i] = (moved - jnp.clip(moved, -0.5, 0.5)).astype(jnp.bfloat16)
            store(i).start()
        for j in range(together):
            i = step * together + j
            total[...] += nt_dot(made[i], full[i])

    left = total[...] - signals[...].astype(jnp.float32)
    misfit_two[...] = left.T.astype(jnp.bfloat16)
    for i in range(blocks):
        store(i).wait()


def slices_of(features):
    unit = features // 12
    ranges, start = [], 0
    for size in (unit, 2 * unit, 2 * unit, unit):
        ranges.append([(start, size), (start + size, size)])
        start += 2 * size
    return ranges


def gaps_of(chips):
    bits = bits_of(chips)
    return [
        (d, b) for d in range(chips) for b in bits
        if any(b in children(d, t, bits) for t in range(TREES))
    ]


def gradient_kernel(
    chips, line, scale, made, misfit, grad,
    core_out, core_in, mine, net_out, net_in, own, z_out, z_in,
    core_send, core_recv, net_send, net_recv, z_send, z_recv,
):
    bits = bits_of(chips)
    gaps = gaps_of(chips)
    slices = slices_of(grad.shape[0])
    me = lax.axis_index("blk")
    z = lax.axis_index("narrow")
    chip, core = me // CORES, me % CORES
    other = CORES * chip + 1 - core
    width = made.shape[2]
    part = grad.shape[1]

    barrier = pltpu.get_barrier_semaphore()
    partners = [other] + [CORES * flip(chip, b) + core for b in bits]
    for partner in partners:
        pl.semaphore_signal(barrier, inc=1, device_id={"blk": partner}, device_id_type=MESH)
    beside = [(z + t) % line for t in range(1, line)]
    for partner in beside:
        pl.semaphore_signal(barrier, inc=1, device_id={"narrow": partner}, device_id_type=MESH)

    def term(d, h, c):
        owner = CORES * flip(chip, d) + (core if c == 0 else 1 - core)
        return jnp.dot(misfit[...], made[owner * UNITS + h], preferred_element_type=jnp.float32)

    def span(k):
        start = slices[k][0][0]
        return start, sum(size for _, size in slices[k])

    def across(d, k):
        rows = pl.ds(*span(k))
        return pltpu.make_async_remote_copy(
            core_out.at[d, rows], core_in.at[d, rows], core_send.at[d, k], core_recv.at[d, k],
            device_id={"blk": other}, device_id_type=MESH,
        )

    def compute(into, d, c):
        for h in range(UNITS):
            into[d, :, h * width:(h + 1) * width] = term(d, h, c).astype(into.dtype)

    def net(d, k, t):
        b = toward(d, t)
        start, size = slices[k][t]
        gap = gaps.index((d ^ b, b))
        rows = pl.ds(start, size)
        return pltpu.make_async_remote_copy(
            net_out.at[d - 1, rows], net_in.at[gap, rows],
            net_send.at[d - 1, k, t], net_recv.at[gap, k, t],
            device_id={"blk": CORES * flip(chip, b) + core}, device_id_type=MESH,
        )

    def summed(d, k, t):
        start, size = slices[k][t]
        value = mine[d, start:start + size] + core_in[d, start:start + size].astype(jnp.float32)
        for b in children(d, t, bits):
            gap = gaps.index((d, b))
            rows = pl.ds(start, size)
            pltpu.make_async_remote_copy(
                net_out.at[0, rows], net_in.at[gap, rows],
                net_send.at[0, k, t], net_recv.at[gap, k, t],
                device_id={"blk": other}, device_id_type=MESH,
            ).wait_recv()
            value += net_in[gap, start:start + size].astype(jnp.float32)
        return value

    def pass_on(d, k, t):
        start, size = slices[k][t]
        net_out[d - 1, start:start + size] = summed(d, k, t).astype(jnp.bfloat16)
        net(d, k, t).start()

    away = sorted(((d, t) for d in range(1, chips) for t in range(TREES)), key=lambda p: -ones(p[0]))
    firsts = [p for p in away if not children(*p, bits)]
    relays = [p for p in away if children(*p, bits)]

    def arrive(k):
        for t in range(TREES):
            start, size = slices[k][t]
            value = summed(0, k, t)
            for j in range(line):
                own[j, start:start + size] = value[:, j * part:(j + 1) * part]

    def z_copy(k, t):
        rows = pl.ds(*span(k))
        return pltpu.make_async_remote_copy(
            z_out.at[t - 1, rows], z_in.at[t - 1, rows], z_send.at[t - 1, k], z_recv.at[t - 1, k],
            device_id={"narrow": (z + t) % line}, device_id_type=MESH,
        )

    def spread(k):
        rows = pl.ds(*span(k))
        for t in range(line - 1, 0, -1):
            z_out[t - 1, rows] = own[(z + t) % line, rows].astype(jnp.bfloat16)
            z_copy(k, t).start()

    def finish(k):
        rows = pl.ds(*span(k))
        value = own[z, rows]
        for t in range(1, line):
            z_copy(k, t).wait_recv()
            value += z_in[t - 1, rows].astype(jnp.float32)
        grad[rows] = value * scale

    order = sorted(range(chips), key=lambda d: (-ones(d), d))
    count = len(slices)
    for i, d in enumerate(order):
        compute(core_out, d, 1)
        if i == 0:
            pl.semaphore_wait(barrier, len(partners) + len(beside))
        across(d, 0).start()
    for d in order:
        across(d, 1).start()

    def begin(d, k):
        across(d, k).wait_recv()
        for e, t in firsts:
            if e == d:
                pass_on(d, k, t)

    for d in order:
        compute(mine, d, 0)
        begin(d, 0)
    for now in range(count + 3):
        if now + 2 < count:
            for d in order:
                across(d, now + 2).start()
        if now < count:
            for d, t in relays:
                pass_on(d, now, t)
        if now + 1 < count:
            for d in order:
                begin(d, now + 1)
        if 1 <= now <= count:
            arrive(now - 1)
            spread(now - 1)
        if now >= 3:
            finish(now - 3)

    for k in range(count):
        for d in order:
            across(d, k).wait_send()
        for d, t in away:
            net(d, k, t).wait_send()
        for t in range(1, line):
            z_copy(k, t).wait_send()


def in_hbm(array):
    return pltpu.with_memory_space_constraint(array, pltpu.HBM)


def body(blk, line, codes, signals, dictionary):
    rows, count = codes.shape
    atoms, features = dictionary.shape
    chips = blk // CORES
    width = atoms // UNITS
    blocks = blk * UNITS
    part = atoms // line
    bf16, f32 = jnp.bfloat16, jnp.float32
    hbm_spec = pl.BlockSpec(memory_space=pltpu.HBM)
    vmem_spec = pl.BlockSpec(memory_space=VMEM)
    flops = 2 * rows * count * features
    size = 2 * rows * count

    full, misfit = pl.pallas_call(
        functools.partial(gather_kernel, chips, line),
        out_shape=(
            jax.ShapeDtypeStruct((blocks, features, width), bf16),
            jax.ShapeDtypeStruct((rows, features), bf16),
        ),
        in_specs=[hbm_spec] * 3,
        out_specs=(vmem_spec, vmem_spec),
        scratch_shapes=[
            VMEM((blocks, rows, width), bf16),
            VMEM((rows, features), bf16),
            VMEM((rows, features), f32),
            DMA((blocks,)), DMA, DMA((UNITS,)),
            DMA((UNITS * max(chips - 1, 1),)), DMA((chips, UNITS)), DMA((chips, TREES)),
            DMA((chips, UNITS)), DMA((chips, UNITS)),
        ],
        compiler_params=pltpu.CompilerParams(
            collective_id=0, has_side_effects=True, vmem_limit_bytes=32 * 2**20
        ),
        cost_estimate=pl.CostEstimate(flops=flops, bytes_accessed=2 * size, transcendentals=0),
        name="gather_atoms",
    )(in_hbm(codes), in_hbm(signals), in_hbm(dictionary.T))

    fresh, made, misfit_two = pl.pallas_call(
        functools.partial(update_kernel, 2 * UNITS),
        out_shape=(
            jax.ShapeDtypeStruct((rows, count), bf16),
            jax.ShapeDtypeStruct((blocks, rows, width), bf16),
            jax.ShapeDtypeStruct((features, rows), bf16),
        ),
        in_specs=[vmem_spec] * 4,
        out_specs=(hbm_spec, vmem_spec, vmem_spec),
        scratch_shapes=[
            VMEM((rows, features), f32),
            DMA((blocks,)),
        ],
        compiler_params=pltpu.CompilerParams(vmem_limit_bytes=24 * 2**20),
        cost_estimate=pl.CostEstimate(flops=2 * flops, bytes_accessed=3 * size, transcendentals=0),
        name="update_codes",
    )(codes, signals, full, misfit)

    gaps = max(len(gaps_of(chips)), 1)
    far = max(chips - 1, 1)
    count_of = len(slices_of(features))
    grad = pl.pallas_call(
        functools.partial(gradient_kernel, chips, line, float(rows * blk * line) ** -0.5),
        out_shape=jax.ShapeDtypeStruct((features, part), f32),
        in_specs=[vmem_spec] * 2,
        out_specs=vmem_spec,
        scratch_shapes=[
            VMEM((chips, features, atoms), bf16),
            VMEM((chips, features, atoms), bf16),
            VMEM((chips, features, atoms), f32),
            VMEM((far, features, atoms), bf16),
            VMEM((gaps, features, atoms), bf16),
            VMEM((line, features, part), f32),
            VMEM((max(line - 1, 1), features, part), bf16),
            VMEM((max(line - 1, 1), features, part), bf16),
            DMA((chips, count_of)), DMA((chips, count_of)),
            DMA((far, count_of, TREES)), DMA((gaps, count_of, TREES)),
            DMA((max(line - 1, 1), count_of)), DMA((max(line - 1, 1), count_of)),
        ],
        compiler_params=pltpu.CompilerParams(
            collective_id=1, has_side_effects=True, vmem_limit_bytes=32 * 2**20
        ),
        cost_estimate=pl.CostEstimate(flops=flops, bytes_accessed=2 * size, transcendentals=0),
        name="dictionary_gradient",
    )(made, misfit_two)
    return fresh, grad.T


def solution(mesh):
    placed = (P(("blk", "narrow"), None), P(("blk", "narrow"), None), P("blk", None))
    return jax.shard_map(
        functools.partial(body, mesh.shape["blk"], mesh.shape["narrow"]),
        mesh=mesh,
        in_specs=placed,
        out_specs=(P(("blk", "narrow"), None), P(("blk", "narrow"), None)),
        check_vma=False,
    )
```

```python
import functools

import jax
import jax.numpy as jnp
from jax import lax
from jax.experimental import pallas as pl
from jax.experimental.pallas import tpu as pltpu
from jax.sharding import PartitionSpec as P

MESH = pl.DeviceIdType.MESH
VMEM = pltpu.VMEM
DMA = pltpu.SemaphoreType.DMA
TREES = 2
UNITS = 6
CORES = 2


def flip(chip, distance):
    bit = 1
    while bit <= distance:
        if distance & bit:
            chip = chip + bit * (1 - 2 * ((chip // bit) % 2))
        bit *= 2
    return chip


def low(d):
    return d & -d


def high(d):
    return 1 << (d.bit_length() - 1)


def ones(d):
    return bin(d).count("1")


def bits_of(chips):
    return [1 << i for i in range(chips.bit_length() - 1)]


def toward(d, half):
    return low(d) if half == 0 else high(d)


def children(d, half, bits):
    return [b for b in bits if d == 0 or (b < low(d) if half == 0 else b > high(d))]


def nt_dot(a, b):
    return lax.dot_general(a, b, (((1,), (1,)), ((), ())), preferred_element_type=jnp.float32)


def gather_kernel(
    chips, line, codes, signals, atoms, full, misfit, held, target, total,
    load_sem, target_sem, atom_sem, net_send, net_recv, pair_send, core_send, core_recv,
):
    bits = bits_of(chips)
    me = lax.axis_index("blk")
    z = lax.axis_index("narrow")
    odd = z % 2
    chip, core = me // CORES, me % CORES
    other = CORES * chip + 1 - core
    width = full.shape[2]
    paired = line % 2 == 0
    lead, rest, late = ([2, 3], [0, 1], [4, 5]) if paired else ([], list(range(UNITS)), [])

    def branches(d, u):
        return [] if u in late else children(d, u % TREES, bits)

    def block(d, u, c):
        unit = u
        if u in lead:
            unit = u + 2 * odd
        if u in late:
            unit = u - 2 * odd
        return (CORES * flip(chip, d) + (core if c == 0 else 1 - core)) * UNITS + unit

    def key(piece):
        return ones(piece[0]), -len(branches(*piece)), piece

    def sort(units, hops):
        return sorted([(d, u) for d in range(1, chips) if ones(d) in hops for u in units], key=key)

    near, distant = [1], range(2, chips)
    order = sort(lead, near) + sort(lead, distant) + sort(rest, near) + sort(late, near)
    order += sort(late, distant) + sort(rest, distant)
    own = [(0, u) for u in range(UNITS)]
    uses = [(d, u, c) for c in range(CORES) for d, u in own]
    uses += [(d, u, c) for d, u in order for c in range(CORES)]

    atom_copies = [
        pltpu.make_async_copy(
            atoms.at[:, pl.ds(u * width, width)], full.at[me * UNITS + u], atom_sem.at[u]
        )
        for u in range(UNITS)
    ]
    for copy in atom_copies:
        copy.start()
    partners = [{"blk": other}] + [{"blk": CORES * flip(chip, b) + core} for b in bits]
    if paired:
        partners.append({"narrow": z + 1 - 2 * odd})
    barrier = pltpu.get_barrier_semaphore()
    for partner in partners:
        pl.semaphore_signal(barrier, inc=1, device_id=partner, device_id_type=MESH)

    def load(slot):
        start = pl.multiple_of(block(*uses[slot]) * width, width)
        return pltpu.make_async_copy(
            codes.at[:, pl.ds(start, width)], held.at[slot], load_sem.at[slot]
        )

    for slot in range(len(uses)):
        load(slot).start()
    target_copy = pltpu.make_async_copy(signals, target, target_sem)
    target_copy.start()

    sends = []

    def net(d, u, b):
        place = full.at[block(d, u, 0)]
        copy = pltpu.make_async_remote_copy(
            place, place, net_send.at[len(sends)], net_recv.at[d ^ b, u],
            device_id={"blk": CORES * flip(chip, b) + core}, device_id_type=MESH,
        )
        copy.start()
        sends.append(copy)

    def pair(d, u):
        place = full.at[block(d, u, 0)]
        return pltpu.make_async_remote_copy(
            place, place, pair_send.at[d, u - lead[0]], net_recv.at[d, u + 2],
            device_id={"narrow": z + 1 - 2 * odd}, device_id_type=MESH,
        )

    def across(d, u, c):
        place = full.at[block(d, u, c)]
        return pltpu.make_async_remote_copy(
            place, place, core_send.at[d, u], core_recv.at[d, u],
            device_id={"blk": other}, device_id_type=MESH,
        )

    def arrived(d, u):
        place = full.at[block(d, u, 0)]
        pltpu.make_async_remote_copy(
            place, place, net_send.at[0], net_recv.at[d, u],
            device_id={"blk": other}, device_id_type=MESH,
        ).wait_recv()

    def use(d, u, c):
        slot = uses.index((d, u, c))
        load(slot).wait()
        total[...] += nt_dot(held[slot], full[block(d, u, c)])

    def send_own(units):
        for step in range(len(units)):
            for i, b in enumerate(bits):
                net(0, units[-1 - step] if i == 0 else units[step], b)

    for copy in atom_copies:
        copy.wait()
    pl.semaphore_wait(barrier, len(partners))
    send_own(lead or rest)
    for d, u in own:
        across(d, u, 0).start()
    total[...] = jnp.zeros_like(total)
    for d, u in own:
        use(d, u, 0)
    waiting = []
    relayed = 0
    for d, u in order:
        arrived(d, u)
        for b in branches(d, u):
            net(d, u, b)
        if u in lead:
            pair(d, u).start()
        across(d, u, 0).start()
        relayed += 1
        if lead and relayed == min(len(bits), len(order)):
            send_own(rest)
        if relayed == max(len(sort(lead, range(chips))), 1):
            for e, v in own:
                across(e, v, 1).wait_recv()
                use(e, v, 1)
        use(d, u, 0)
        waiting.append((d, u))
        if len(waiting) > 2:
            e, v = waiting.pop(0)
            across(e, v, 1).wait_recv()
            use(e, v, 1)
    for e, v in waiting:
        across(e, v, 1).wait_recv()
        use(e, v, 1)
    target_copy.wait()
    rounded = (total[...] - target[...].astype(jnp.float32)).astype(jnp.bfloat16)
    misfit[...] = (rounded.astype(jnp.float32) * -4.0).astype(jnp.bfloat16)
    for copy in sends:
        copy.wait_send()
    for d, u in own + order:
        across(d, u, 0).wait_send()
        if d and u in lead:
            pair(d, u).wait_send()


def update_kernel(together, codes, signals, full, misfit, fresh, made, misfit_two, total, store_sem):
    blocks, _, width = full.shape

    def store(i):
        start = pl.multiple_of(i * width, width)
        return pltpu.make_async_copy(
            made.at[i], fresh.at[:, pl.ds(start, width)], store_sem.at[i]
        )

    total[...] = jnp.zeros_like(total)

    @pl.loop(0, blocks // together)
    def _(step):
        for j in range(together):
            i = step * together + j
            start = pl.multiple_of(i * width, width)
            change = jnp.dot(misfit[...], full[i], preferred_element_type=jnp.float32)
            moved = codes[:, pl.ds(start, width)].astype(jnp.float32) + change
            made[i] = (moved - jnp.clip(moved, -0.5, 0.5)).astype(jnp.bfloat16)
            store(i).start()
        value = total[...]
        for j in range(together):
            i = step * together + j
            value += nt_dot(made[i], full[i])
        total[...] = value

    left = total[...] - signals[...].astype(jnp.float32)
    misfit_two[...] = left.T.astype(jnp.bfloat16)
    for i in range(blocks):
        store(i).wait()


def slices_of(features):
    size = features // 12
    return [[(start, size), (start + size, size)] for start in range(0, features, 2 * size)]


def gaps_of(chips):
    bits = bits_of(chips)
    return [
        (d, b) for d in range(chips) for b in bits
        if any(b in children(d, t, bits) for t in range(TREES))
    ]


def gradient_kernel(
    chips, line, scale, made, misfit, grad,
    core_out, core_in, mine, net_out, net_in, own, z_out, z_in,
    core_send, core_recv, net_send, net_recv, z_send, z_recv,
):
    bits = bits_of(chips)
    gaps = gaps_of(chips)
    slices = slices_of(grad.shape[0])
    me = lax.axis_index("blk")
    z = lax.axis_index("narrow")
    chip, core = me // CORES, me % CORES
    other = CORES * chip + 1 - core
    width = made.shape[2]
    part = grad.shape[1]

    barrier = pltpu.get_barrier_semaphore()
    partners = [other] + [CORES * flip(chip, b) + core for b in bits]
    for partner in partners:
        pl.semaphore_signal(barrier, inc=1, device_id={"blk": partner}, device_id_type=MESH)
    beside = [(z + t) % line for t in range(1, line)]
    for partner in beside:
        pl.semaphore_signal(barrier, inc=1, device_id={"narrow": partner}, device_id_type=MESH)

    def term(d, h, c):
        owner = CORES * flip(chip, d) + (core if c == 0 else 1 - core)
        return jnp.dot(misfit[...], made[owner * UNITS + h], preferred_element_type=jnp.float32)

    def span(k):
        start = slices[k][0][0]
        return start, sum(size for _, size in slices[k])

    def across(d, k):
        rows = pl.ds(*span(k))
        return pltpu.make_async_remote_copy(
            core_out.at[d, rows], core_in.at[d, rows], core_send.at[d, k], core_recv.at[d, k],
            device_id={"blk": other}, device_id_type=MESH,
        )

    def compute(into, d, c):
        for h in range(UNITS):
            into[d, :, h * width:(h + 1) * width] = term(d, h, c).astype(into.dtype)

    def net(d, k, t):
        b = toward(d, t)
        start, size = slices[k][t]
        gap = gaps.index((d ^ b, b))
        rows = pl.ds(start, size)
        return pltpu.make_async_remote_copy(
            net_out.at[d - 1, rows], net_in.at[gap, rows],
            net_send.at[d - 1, k, t], net_recv.at[gap, k, t],
            device_id={"blk": CORES * flip(chip, b) + core}, device_id_type=MESH,
        )

    def summed(d, k, t):
        start, size = slices[k][t]
        value = mine[d, start:start + size] + core_in[d, start:start + size].astype(jnp.float32)
        for b in children(d, t, bits):
            gap = gaps.index((d, b))
            rows = pl.ds(start, size)
            pltpu.make_async_remote_copy(
                net_out.at[0, rows], net_in.at[gap, rows],
                net_send.at[0, k, t], net_recv.at[gap, k, t],
                device_id={"blk": other}, device_id_type=MESH,
            ).wait_recv()
            value += net_in[gap, start:start + size].astype(jnp.float32)
        return value

    def pass_on(d, k, t):
        start, size = slices[k][t]
        net_out[d - 1, start:start + size] = summed(d, k, t).astype(jnp.bfloat16)
        net(d, k, t).start()

    away = sorted(((d, t) for d in range(1, chips) for t in range(TREES)), key=lambda p: -ones(p[0]))
    firsts = [p for p in away if not children(*p, bits)]
    relays = [p for p in away if children(*p, bits)]

    def arrive(k):
        for t in range(TREES):
            start, size = slices[k][t]
            value = summed(0, k, t)
            for j in range(line):
                own[j, start:start + size] = value[:, j * part:(j + 1) * part]

    def z_copy(k, t):
        rows = pl.ds(*span(k))
        return pltpu.make_async_remote_copy(
            z_out.at[t - 1, rows], z_in.at[t - 1, rows], z_send.at[t - 1, k], z_recv.at[t - 1, k],
            device_id={"narrow": (z + t) % line}, device_id_type=MESH,
        )

    def spread(k):
        rows = pl.ds(*span(k))
        for t in range(line - 1, 0, -1):
            z_out[t - 1, rows] = own[(z + t) % line, rows].astype(jnp.bfloat16)
            z_copy(k, t).start()

    def finish(k):
        rows = pl.ds(*span(k))
        value = own[z, rows]
        for t in range(1, line):
            z_copy(k, t).wait_recv()
            value += z_in[t - 1, rows].astype(jnp.float32)
        grad[rows] = value * scale

    order = sorted(range(chips), key=lambda d: (-ones(d), d))
    count = len(slices)
    for i, d in enumerate(order):
        compute(core_out, d, 1)
        if i == 0:
            pl.semaphore_wait(barrier, len(partners) + len(beside))
        across(d, 0).start()
    for d in order:
        across(d, 1).start()

    def begin(d, k):
        across(d, k).wait_recv()
        for e, t in firsts:
            if e == d:
                pass_on(d, k, t)

    for d in order:
        compute(mine, d, 0)
        begin(d, 0)
    for now in range(count + 3):
        if now + 2 < count:
            for d in order:
                across(d, now + 2).start()
        if now < count:
            for d, t in relays:
                pass_on(d, now, t)
        if now + 1 < count:
            for d in order:
                begin(d, now + 1)
        if 1 <= now <= count:
            arrive(now - 1)
            spread(now - 1)
        if now >= 3:
            finish(now - 3)

    for k in range(count):
        for d in order:
            across(d, k).wait_send()
        for d, t in away:
            net(d, k, t).wait_send()
        for t in range(1, line):
            z_copy(k, t).wait_send()


def in_hbm(array):
    return pltpu.with_memory_space_constraint(array, pltpu.HBM)


def body(blk, line, codes, signals, dictionary):
    rows, count = codes.shape
    atoms, features = dictionary.shape
    chips = blk // CORES
    width = atoms // UNITS
    blocks = blk * UNITS
    part = atoms // line
    bf16, f32 = jnp.bfloat16, jnp.float32
    hbm_spec = pl.BlockSpec(memory_space=pltpu.HBM)
    vmem_spec = pl.BlockSpec(memory_space=VMEM)
    flops = 2 * rows * count * features
    size = 2 * rows * count

    full, misfit = pl.pallas_call(
        functools.partial(gather_kernel, chips, line),
        out_shape=(
            jax.ShapeDtypeStruct((blocks, features, width), bf16),
            jax.ShapeDtypeStruct((rows, features), bf16),
        ),
        in_specs=[hbm_spec] * 3,
        out_specs=(vmem_spec, vmem_spec),
        scratch_shapes=[
            VMEM((blocks, rows, width), bf16),
            VMEM((rows, features), bf16),
            VMEM((rows, features), f32),
            DMA((blocks,)), DMA, DMA((UNITS,)),
            DMA((UNITS * max(chips - 1, 1),)), DMA((chips, UNITS)), DMA((chips, TREES)),
            DMA((chips, UNITS)), DMA((chips, UNITS)),
        ],
        compiler_params=pltpu.CompilerParams(
            collective_id=0, has_side_effects=True, vmem_limit_bytes=32 * 2**20
        ),
        cost_estimate=pl.CostEstimate(flops=flops, bytes_accessed=2 * size, transcendentals=0),
        name="gather_atoms",
    )(in_hbm(codes), in_hbm(signals), in_hbm(dictionary.T))

    fresh, made, misfit_two = pl.pallas_call(
        functools.partial(update_kernel, 2 * UNITS),
        out_shape=(
            jax.ShapeDtypeStruct((rows, count), bf16),
            jax.ShapeDtypeStruct((blocks, rows, width), bf16),
            jax.ShapeDtypeStruct((features, rows), bf16),
        ),
        in_specs=[vmem_spec] * 4,
        out_specs=(hbm_spec, vmem_spec, vmem_spec),
        scratch_shapes=[
            VMEM((rows, features), f32),
            DMA((blocks,)),
        ],
        compiler_params=pltpu.CompilerParams(vmem_limit_bytes=24 * 2**20),
        cost_estimate=pl.CostEstimate(flops=2 * flops, bytes_accessed=3 * size, transcendentals=0),
        name="update_codes",
    )(codes, signals, full, misfit)

    gaps = max(len(gaps_of(chips)), 1)
    far = max(chips - 1, 1)
    count_of = len(slices_of(features))
    grad = pl.pallas_call(
        functools.partial(gradient_kernel, chips, line, float(rows * blk * line) ** -0.5),
        out_shape=jax.ShapeDtypeStruct((features, part), f32),
        in_specs=[vmem_spec] * 2,
        out_specs=vmem_spec,
        scratch_shapes=[
            VMEM((chips, features, atoms), bf16),
            VMEM((chips, features, atoms), bf16),
            VMEM((chips, features, atoms), f32),
            VMEM((far, features, atoms), bf16),
            VMEM((gaps, features, atoms), bf16),
            VMEM((line, features, part), f32),
            VMEM((max(line - 1, 1), features, part), bf16),
            VMEM((max(line - 1, 1), features, part), bf16),
            DMA((chips, count_of)), DMA((chips, count_of)),
            DMA((far, count_of, TREES)), DMA((gaps, count_of, TREES)),
            DMA((max(line - 1, 1), count_of)), DMA((max(line - 1, 1), count_of)),
        ],
        compiler_params=pltpu.CompilerParams(
            collective_id=1, has_side_effects=True, vmem_limit_bytes=32 * 2**20
        ),
        cost_estimate=pl.CostEstimate(flops=flops, bytes_accessed=2 * size, transcendentals=0),
        name="dictionary_gradient",
    )(made, misfit_two)
    return fresh, grad.T


def solution(mesh):
    placed = (P(("blk", "narrow"), None), P(("blk", "narrow"), None), P("blk", None))
    return jax.shard_map(
        functools.partial(body, mesh.shape["blk"], mesh.shape["narrow"]),
        mesh=mesh,
        in_specs=placed,
        out_specs=(P(("blk", "narrow"), None), P(("blk", "narrow"), None)),
        check_vma=False,
    )
```

```python
import functools

import jax
import jax.numpy as jnp
from jax import lax
from jax.experimental import pallas as pl
from jax.experimental.pallas import tpu as pltpu
from jax.sharding import PartitionSpec as P

MESH = pl.DeviceIdType.MESH
VMEM = pltpu.VMEM
DMA = pltpu.SemaphoreType.DMA
TREES = 2
UNITS = 6
CORES = 2


def flip(chip, distance):
    bit = 1
    while bit <= distance:
        if distance & bit:
            chip = chip + bit * (1 - 2 * ((chip // bit) % 2))
        bit *= 2
    return chip


def low(d):
    return d & -d


def high(d):
    return 1 << (d.bit_length() - 1)


def ones(d):
    return bin(d).count("1")


def bits_of(chips):
    return [1 << i for i in range(chips.bit_length() - 1)]


def toward(d, half):
    return low(d) if half == 0 else high(d)


def children(d, half, bits):
    return [b for b in bits if d == 0 or (b < low(d) if half == 0 else b > high(d))]


def nt_dot(a, b):
    return lax.dot_general(a, b, (((1,), (1,)), ((), ())), preferred_element_type=jnp.float32)


def gather_kernel(
    chips, line, codes, signals, atoms, full, misfit, held, target, total,
    load_sem, target_sem, atom_sem, net_send, net_recv, pair_send, core_send, core_recv,
):
    bits = bits_of(chips)
    me = lax.axis_index("blk")
    z = lax.axis_index("narrow")
    odd = z % 2
    chip, core = me // CORES, me % CORES
    other = CORES * chip + 1 - core
    width = full.shape[2]
    paired = line % 2 == 0
    lead, rest, late = ([2, 3], [0, 1], [4, 5]) if paired else ([], list(range(UNITS)), [])

    def branches(d, u):
        return [] if u in late else children(d, u % TREES, bits)

    def block(d, u, c):
        unit = u
        if u in lead:
            unit = u + 2 * odd
        if u in late:
            unit = u - 2 * odd
        return (CORES * flip(chip, d) + (core if c == 0 else 1 - core)) * UNITS + unit

    def key(piece):
        return ones(piece[0]), -len(branches(*piece)), piece

    def sort(units, hops):
        return sorted([(d, u) for d in range(1, chips) if ones(d) in hops for u in units], key=key)

    near, distant = [1], range(2, chips)
    order = sort(lead, near) + sort(lead, distant) + sort(rest, near) + sort(late, near)
    order += sort(late, distant) + sort(rest, distant)
    own = [(0, u) for u in range(UNITS)]
    uses = [(d, u, c) for c in range(CORES) for d, u in own]
    uses += [(d, u, c) for d, u in order for c in range(CORES)]

    atom_copies = [
        pltpu.make_async_copy(
            atoms.at[:, pl.ds(u * width, width)], full.at[me * UNITS + u], atom_sem.at[u]
        )
        for u in range(UNITS)
    ]
    for copy in atom_copies:
        copy.start()
    partners = [{"blk": other}] + [{"blk": CORES * flip(chip, b) + core} for b in bits]
    if paired:
        partners.append({"narrow": z + 1 - 2 * odd})
    barrier = pltpu.get_barrier_semaphore()
    for partner in partners:
        pl.semaphore_signal(barrier, inc=1, device_id=partner, device_id_type=MESH)

    def load(slot):
        start = pl.multiple_of(block(*uses[slot]) * width, width)
        return pltpu.make_async_copy(
            codes.at[:, pl.ds(start, width)], held.at[slot], load_sem.at[slot]
        )

    for slot in range(len(uses)):
        load(slot).start()
    target_copy = pltpu.make_async_copy(signals, target, target_sem)
    target_copy.start()

    sends = []

    def net(d, u, b):
        place = full.at[block(d, u, 0)]
        copy = pltpu.make_async_remote_copy(
            place, place, net_send.at[len(sends)], net_recv.at[d ^ b, u],
            device_id={"blk": CORES * flip(chip, b) + core}, device_id_type=MESH,
        )
        copy.start()
        sends.append(copy)

    def pair(d, u):
        place = full.at[block(d, u, 0)]
        return pltpu.make_async_remote_copy(
            place, place, pair_send.at[d, u - lead[0]], net_recv.at[d, u + 2],
            device_id={"narrow": z + 1 - 2 * odd}, device_id_type=MESH,
        )

    def across(d, u, c):
        place = full.at[block(d, u, c)]
        return pltpu.make_async_remote_copy(
            place, place, core_send.at[d, u], core_recv.at[d, u],
            device_id={"blk": other}, device_id_type=MESH,
        )

    def arrived(d, u):
        place = full.at[block(d, u, 0)]
        pltpu.make_async_remote_copy(
            place, place, net_send.at[0], net_recv.at[d, u],
            device_id={"blk": other}, device_id_type=MESH,
        ).wait_recv()

    def use(d, u, c):
        slot = uses.index((d, u, c))
        load(slot).wait()
        total[...] += nt_dot(held[slot], full[block(d, u, c)])

    def send_own(units):
        for step in range(len(units)):
            for i, b in enumerate(bits):
                net(0, units[-1 - step] if i == 0 else units[step], b)

    for copy in atom_copies:
        copy.wait()
    pl.semaphore_wait(barrier, len(partners))
    send_own(lead or rest)
    for d, u in own:
        across(d, u, 0).start()
    total[...] = jnp.zeros_like(total)
    for d, u in own:
        use(d, u, 0)
    waiting = []
    relayed = 0
    for d, u in order:
        arrived(d, u)
        for b in branches(d, u):
            net(d, u, b)
        if u in lead:
            pair(d, u).start()
        across(d, u, 0).start()
        relayed += 1
        if lead and relayed == min(len(bits), len(order)):
            send_own(rest)
        if relayed == max(len(sort(lead, range(chips))), 1):
            for e, v in own:
                across(e, v, 1).wait_recv()
                use(e, v, 1)
        use(d, u, 0)
        waiting.append((d, u))
        if len(waiting) > 2:
            e, v = waiting.pop(0)
            across(e, v, 1).wait_recv()
            use(e, v, 1)
    for e, v in waiting:
        across(e, v, 1).wait_recv()
        use(e, v, 1)
    target_copy.wait()
    rounded = (total[...] - target[...].astype(jnp.float32)).astype(jnp.bfloat16)
    misfit[...] = (rounded.astype(jnp.float32) * -4.0).astype(jnp.bfloat16)
    for copy in sends:
        copy.wait_send()
    for d, u in own + order:
        across(d, u, 0).wait_send()
        if d and u in lead:
            pair(d, u).wait_send()


def update_kernel(together, codes, signals, full, misfit, fresh, made, misfit_two, total, store_sem):
    blocks, _, width = full.shape

    def store(i):
        start = pl.multiple_of(i * width, width)
        return pltpu.make_async_copy(
            made.at[i], fresh.at[:, pl.ds(start, width)], store_sem.at[i]
        )

    total[...] = jnp.zeros_like(total)

    @pl.loop(0, blocks // together)
    def _(step):
        for j in range(together):
            i = step * together + j
            start = pl.multiple_of(i * width, width)
            change = jnp.dot(misfit[...], full[i], preferred_element_type=jnp.float32)
            moved = codes[:, pl.ds(start, width)].astype(jnp.float32) + change
            made[i] = (moved - jnp.clip(moved, -0.5, 0.5)).astype(jnp.bfloat16)
            store(i).start()
        value = total[...]
        for j in range(together):
            i = step * together + j
            value += nt_dot(made[i], full[i])
        total[...] = value

    left = total[...] - signals[...].astype(jnp.float32)
    misfit_two[...] = left.T.astype(jnp.bfloat16)
    for i in range(blocks):
        store(i).wait()


def slices_of(features):
    size = features // 6
    return [[(start, size), (start + size, size)] for start in range(0, features, 2 * size)]


def gaps_of(chips):
    bits = bits_of(chips)
    return [
        (d, b) for d in range(chips) for b in bits
        if any(b in children(d, t, bits) for t in range(TREES))
    ]


def gradient_kernel(
    chips, line, scale, made, misfit, grad,
    core_out, core_in, mine, net_out, net_in, own, z_out, z_in,
    core_send, core_recv, net_send, net_recv, z_send, z_recv,
):
    bits = bits_of(chips)
    gaps = gaps_of(chips)
    slices = slices_of(grad.shape[0])
    me = lax.axis_index("blk")
    z = lax.axis_index("narrow")
    chip, core = me // CORES, me % CORES
    other = CORES * chip + 1 - core
    width = made.shape[2]
    part = grad.shape[1]

    barrier = pltpu.get_barrier_semaphore()
    partners = [other] + [CORES * flip(chip, b) + core for b in bits]
    for partner in partners:
        pl.semaphore_signal(barrier, inc=1, device_id={"blk": partner}, device_id_type=MESH)
    beside = [(z + t) % line for t in range(1, line)]
    for partner in beside:
        pl.semaphore_signal(barrier, inc=1, device_id={"narrow": partner}, device_id_type=MESH)

    def term(d, h, c):
        owner = CORES * flip(chip, d) + (core if c == 0 else 1 - core)
        return jnp.dot(misfit[...], made[owner * UNITS + h], preferred_element_type=jnp.float32)

    def span(k):
        start = slices[k][0][0]
        return start, sum(size for _, size in slices[k])

    def across(d, k):
        rows = pl.ds(*span(k))
        return pltpu.make_async_remote_copy(
            core_out.at[d, rows], core_in.at[d, rows], core_send.at[d, k], core_recv.at[d, k],
            device_id={"blk": other}, device_id_type=MESH,
        )

    def compute(into, d, c):
        for h in range(UNITS):
            into[d, :, h * width:(h + 1) * width] = term(d, h, c).astype(into.dtype)

    def net(d, k, t):
        b = toward(d, t)
        start, size = slices[k][t]
        gap = gaps.index((d ^ b, b))
        rows = pl.ds(start, size)
        return pltpu.make_async_remote_copy(
            net_out.at[d - 1, rows], net_in.at[gap, rows],
            net_send.at[d - 1, k, t], net_recv.at[gap, k, t],
            device_id={"blk": CORES * flip(chip, b) + core}, device_id_type=MESH,
        )

    def summed(d, k, t):
        start, size = slices[k][t]
        value = mine[d, start:start + size] + core_in[d, start:start + size].astype(jnp.float32)
        for b in children(d, t, bits):
            gap = gaps.index((d, b))
            rows = pl.ds(start, size)
            pltpu.make_async_remote_copy(
                net_out.at[0, rows], net_in.at[gap, rows],
                net_send.at[0, k, t], net_recv.at[gap, k, t],
                device_id={"blk": other}, device_id_type=MESH,
            ).wait_recv()
            value += net_in[gap, start:start + size].astype(jnp.float32)
        return value

    def pass_on(d, k, t):
        start, size = slices[k][t]
        net_out[d - 1, start:start + size] = summed(d, k, t).astype(jnp.bfloat16)
        net(d, k, t).start()

    away = sorted(((d, t) for d in range(1, chips) for t in range(TREES)), key=lambda p: -ones(p[0]))
    firsts = [p for p in away if not children(*p, bits)]
    relays = [p for p in away if children(*p, bits)]

    def arrive(k):
        for t in range(TREES):
            start, size = slices[k][t]
            value = summed(0, k, t)
            for j in range(line):
                own[j, start:start + size] = value[:, j * part:(j + 1) * part]

    def z_copy(k, t):
        rows = pl.ds(*span(k))
        return pltpu.make_async_remote_copy(
            z_out.at[t - 1, rows], z_in.at[t - 1, rows], z_send.at[t - 1, k], z_recv.at[t - 1, k],
            device_id={"narrow": (z + t) % line}, device_id_type=MESH,
        )

    def spread(k):
        rows = pl.ds(*span(k))
        for t in range(line - 1, 0, -1):
            z_out[t - 1, rows] = own[(z + t) % line, rows].astype(jnp.bfloat16)
            z_copy(k, t).start()

    def finish(k):
        rows = pl.ds(*span(k))
        value = own[z, rows]
        for t in range(1, line):
            z_copy(k, t).wait_recv()
            value += z_in[t - 1, rows].astype(jnp.float32)
        grad[rows] = value * scale

    order = sorted(range(chips), key=lambda d: (-ones(d), d))
    count = len(slices)
    for i, d in enumerate(order):
        compute(core_out, d, 1)
        if i == 0:
            pl.semaphore_wait(barrier, len(partners) + len(beside))
        across(d, 0).start()
    for d in order:
        across(d, 1).start()

    def begin(d, k):
        across(d, k).wait_recv()
        for e, t in firsts:
            if e == d:
                pass_on(d, k, t)

    for d in order:
        compute(mine, d, 0)
        begin(d, 0)
    for now in range(count + 3):
        if now + 2 < count:
            for d in order:
                across(d, now + 2).start()
        if now < count:
            for d, t in relays:
                pass_on(d, now, t)
        if now + 1 < count:
            for d in order:
                begin(d, now + 1)
        if 1 <= now <= count:
            arrive(now - 1)
            spread(now - 1)
        if now >= 3:
            finish(now - 3)

    for k in range(count):
        for d in order:
            across(d, k).wait_send()
        for d, t in away:
            net(d, k, t).wait_send()
        for t in range(1, line):
            z_copy(k, t).wait_send()


def in_hbm(array):
    return pltpu.with_memory_space_constraint(array, pltpu.HBM)


def body(blk, line, codes, signals, dictionary):
    rows, count = codes.shape
    atoms, features = dictionary.shape
    chips = blk // CORES
    width = atoms // UNITS
    blocks = blk * UNITS
    part = atoms // line
    bf16, f32 = jnp.bfloat16, jnp.float32
    hbm_spec = pl.BlockSpec(memory_space=pltpu.HBM)
    vmem_spec = pl.BlockSpec(memory_space=VMEM)
    flops = 2 * rows * count * features
    size = 2 * rows * count

    full, misfit = pl.pallas_call(
        functools.partial(gather_kernel, chips, line),
        out_shape=(
            jax.ShapeDtypeStruct((blocks, features, width), bf16),
            jax.ShapeDtypeStruct((rows, features), bf16),
        ),
        in_specs=[hbm_spec] * 3,
        out_specs=(vmem_spec, vmem_spec),
        scratch_shapes=[
            VMEM((blocks, rows, width), bf16),
            VMEM((rows, features), bf16),
            VMEM((rows, features), f32),
            DMA((blocks,)), DMA, DMA((UNITS,)),
            DMA((UNITS * max(chips - 1, 1),)), DMA((chips, UNITS)), DMA((chips, TREES)),
            DMA((chips, UNITS)), DMA((chips, UNITS)),
        ],
        compiler_params=pltpu.CompilerParams(
            collective_id=0, has_side_effects=True, vmem_limit_bytes=32 * 2**20
        ),
        cost_estimate=pl.CostEstimate(flops=flops, bytes_accessed=2 * size, transcendentals=0),
        name="gather_atoms",
    )(in_hbm(codes), in_hbm(signals), in_hbm(dictionary.T))

    fresh, made, misfit_two = pl.pallas_call(
        functools.partial(update_kernel, 2 * UNITS),
        out_shape=(
            jax.ShapeDtypeStruct((rows, count), bf16),
            jax.ShapeDtypeStruct((blocks, rows, width), bf16),
            jax.ShapeDtypeStruct((features, rows), bf16),
        ),
        in_specs=[vmem_spec] * 4,
        out_specs=(hbm_spec, vmem_spec, vmem_spec),
        scratch_shapes=[
            VMEM((rows, features), f32),
            DMA((blocks,)),
        ],
        compiler_params=pltpu.CompilerParams(vmem_limit_bytes=24 * 2**20),
        cost_estimate=pl.CostEstimate(flops=2 * flops, bytes_accessed=3 * size, transcendentals=0),
        name="update_codes",
    )(codes, signals, full, misfit)

    gaps = max(len(gaps_of(chips)), 1)
    far = max(chips - 1, 1)
    count_of = len(slices_of(features))
    grad = pl.pallas_call(
        functools.partial(gradient_kernel, chips, line, float(rows * blk * line) ** -0.5),
        out_shape=jax.ShapeDtypeStruct((features, part), f32),
        in_specs=[vmem_spec] * 2,
        out_specs=vmem_spec,
        scratch_shapes=[
            VMEM((chips, features, atoms), bf16),
            VMEM((chips, features, atoms), bf16),
            VMEM((chips, features, atoms), f32),
            VMEM((far, features, atoms), bf16),
            VMEM((gaps, features, atoms), bf16),
            VMEM((line, features, part), f32),
            VMEM((max(line - 1, 1), features, part), bf16),
            VMEM((max(line - 1, 1), features, part), bf16),
            DMA((chips, count_of)), DMA((chips, count_of)),
            DMA((far, count_of, TREES)), DMA((gaps, count_of, TREES)),
            DMA((max(line - 1, 1), count_of)), DMA((max(line - 1, 1), count_of)),
        ],
        compiler_params=pltpu.CompilerParams(
            collective_id=1, has_side_effects=True, vmem_limit_bytes=32 * 2**20
        ),
        cost_estimate=pl.CostEstimate(flops=flops, bytes_accessed=2 * size, transcendentals=0),
        name="dictionary_gradient",
    )(made, misfit_two)
    return fresh, grad.T


def solution(mesh):
    placed = (P(("blk", "narrow"), None), P(("blk", "narrow"), None), P("blk", None))
    return jax.shard_map(
        functools.partial(body, mesh.shape["blk"], mesh.shape["narrow"]),
        mesh=mesh,
        in_specs=placed,
        out_specs=(P(("blk", "narrow"), None), P(("blk", "narrow"), None)),
        check_vma=False,
    )
```

```python
import functools

import jax
import jax.numpy as jnp
from jax import lax
from jax.experimental import pallas as pl
from jax.experimental.pallas import tpu as pltpu
from jax.sharding import PartitionSpec as P

MESH = pl.DeviceIdType.MESH
VMEM = pltpu.VMEM
DMA = pltpu.SemaphoreType.DMA
TREES = 2
UNITS = 6
CORES = 2


def flip(chip, distance):
    bit = 1
    while bit <= distance:
        if distance & bit:
            chip = chip + bit * (1 - 2 * ((chip // bit) % 2))
        bit *= 2
    return chip


def low(d):
    return d & -d


def high(d):
    return 1 << (d.bit_length() - 1)


def ones(d):
    return bin(d).count("1")


def bits_of(chips):
    return [1 << i for i in range(chips.bit_length() - 1)]


def toward(d, half):
    return low(d) if half == 0 else high(d)


def children(d, half, bits):
    return [b for b in bits if d == 0 or (b < low(d) if half == 0 else b > high(d))]


def nt_dot(a, b):
    return lax.dot_general(a, b, (((1,), (1,)), ((), ())), preferred_element_type=jnp.float32)


def gather_kernel(
    chips, line, codes, signals, atoms, full, misfit, held, target, total,
    load_sem, target_sem, atom_sem, net_send, net_recv, pair_send, core_send, core_recv,
):
    bits = bits_of(chips)
    me = lax.axis_index("blk")
    z = lax.axis_index("narrow")
    odd = z % 2
    chip, core = me // CORES, me % CORES
    other = CORES * chip + 1 - core
    width = full.shape[2]
    paired = line % 2 == 0
    lead, rest, late = ([2, 3], [0, 1], [4, 5]) if paired else ([], list(range(UNITS)), [])

    def branches(d, u):
        return [] if u in late else children(d, u % TREES, bits)

    def block(d, u, c):
        unit = u
        if u in lead:
            unit = u + 2 * odd
        if u in late:
            unit = u - 2 * odd
        return (CORES * flip(chip, d) + (core if c == 0 else 1 - core)) * UNITS + unit

    def key(piece):
        return ones(piece[0]), -len(branches(*piece)), piece

    def sort(units, hops):
        return sorted([(d, u) for d in range(1, chips) if ones(d) in hops for u in units], key=key)

    near, distant = [1], range(2, chips)
    order = sort(lead, near) + sort(lead, distant) + sort(rest, near) + sort(late, near)
    order += sort(late, distant) + sort(rest, distant)
    own = [(0, u) for u in range(UNITS)]
    uses = [(d, u, c) for c in range(CORES) for d, u in own]
    uses += [(d, u, c) for d, u in order for c in range(CORES)]

    atom_copies = [
        pltpu.make_async_copy(
            atoms.at[:, pl.ds(u * width, width)], full.at[me * UNITS + u], atom_sem.at[u]
        )
        for u in range(UNITS)
    ]
    for copy in atom_copies:
        copy.start()
    partners = [{"blk": other}] + [{"blk": CORES * flip(chip, b) + core} for b in bits]
    if paired:
        partners.append({"narrow": z + 1 - 2 * odd})
    barrier = pltpu.get_barrier_semaphore()
    for partner in partners:
        pl.semaphore_signal(barrier, inc=1, device_id=partner, device_id_type=MESH)

    def load(slot):
        start = pl.multiple_of(block(*uses[slot]) * width, width)
        return pltpu.make_async_copy(
            codes.at[:, pl.ds(start, width)], held.at[slot], load_sem.at[slot]
        )

    for slot in range(len(uses)):
        load(slot).start()
    target_copy = pltpu.make_async_copy(signals, target, target_sem)
    target_copy.start()

    sends = []

    def net(d, u, b):
        place = full.at[block(d, u, 0)]
        copy = pltpu.make_async_remote_copy(
            place, place, net_send.at[len(sends)], net_recv.at[d ^ b, u],
            device_id={"blk": CORES * flip(chip, b) + core}, device_id_type=MESH,
        )
        copy.start()
        sends.append(copy)

    def pair(d, u):
        place = full.at[block(d, u, 0)]
        return pltpu.make_async_remote_copy(
            place, place, pair_send.at[d, u - lead[0]], net_recv.at[d, u + 2],
            device_id={"narrow": z + 1 - 2 * odd}, device_id_type=MESH,
        )

    def across(d, u, c):
        place = full.at[block(d, u, c)]
        return pltpu.make_async_remote_copy(
            place, place, core_send.at[d, u], core_recv.at[d, u],
            device_id={"blk": other}, device_id_type=MESH,
        )

    def arrived(d, u):
        place = full.at[block(d, u, 0)]
        pltpu.make_async_remote_copy(
            place, place, net_send.at[0], net_recv.at[d, u],
            device_id={"blk": other}, device_id_type=MESH,
        ).wait_recv()

    def use(d, u, c):
        slot = uses.index((d, u, c))
        load(slot).wait()
        total[...] += nt_dot(held[slot], full[block(d, u, c)])

    def send_own(units):
        for step in range(len(units)):
            for i, b in enumerate(bits):
                net(0, units[-1 - step] if i == 0 else units[step], b)

    for copy in atom_copies:
        copy.wait()
    pl.semaphore_wait(barrier, len(partners))
    send_own(lead or rest)
    for d, u in own:
        across(d, u, 0).start()
    total[...] = jnp.zeros_like(total)
    for d, u in own:
        use(d, u, 0)
    waiting = []
    relayed = 0
    for d, u in order:
        arrived(d, u)
        for b in branches(d, u):
            net(d, u, b)
        if u in lead:
            pair(d, u).start()
        across(d, u, 0).start()
        relayed += 1
        if lead and relayed == min(len(bits), len(order)):
            send_own(rest)
        if relayed == max(len(sort(lead, range(chips))), 1):
            for e, v in own:
                across(e, v, 1).wait_recv()
                use(e, v, 1)
        use(d, u, 0)
        waiting.append((d, u))
        if len(waiting) > 2:
            e, v = waiting.pop(0)
            across(e, v, 1).wait_recv()
            use(e, v, 1)
    for e, v in waiting:
        across(e, v, 1).wait_recv()
        use(e, v, 1)
    target_copy.wait()
    rounded = (total[...] - target[...].astype(jnp.float32)).astype(jnp.bfloat16)
    misfit[...] = (rounded.astype(jnp.float32) * -4.0).astype(jnp.bfloat16)
    for copy in sends:
        copy.wait_send()
    for d, u in own + order:
        across(d, u, 0).wait_send()
        if d and u in lead:
            pair(d, u).wait_send()


def update_kernel(together, codes, signals, full, misfit, fresh, made, misfit_two, total, store_sem):
    blocks, _, width = full.shape

    def store(i):
        start = pl.multiple_of(i * width, width)
        return pltpu.make_async_copy(
            made.at[i], fresh.at[:, pl.ds(start, width)], store_sem.at[i]
        )

    total[...] = jnp.zeros_like(total)

    @pl.loop(0, blocks // together)
    def _(step):
        for j in range(together):
            i = step * together + j
            start = pl.multiple_of(i * width, width)
            change = jnp.dot(misfit[...], full[i], preferred_element_type=jnp.float32)
            moved = codes[:, pl.ds(start, width)].astype(jnp.float32) + change
            made[i] = (moved - jnp.clip(moved, -0.5, 0.5)).astype(jnp.bfloat16)
            store(i).start()
        value = total[...]
        for j in range(together):
            i = step * together + j
            value += nt_dot(made[i], full[i])
        total[...] = value

    left = total[...] - signals[...].astype(jnp.float32)
    misfit_two[...] = left.T.astype(jnp.bfloat16)
    for i in range(blocks):
        store(i).wait()


def slices_of(features):
    unit = features // 12
    ranges, start = [], 0
    for size in (2 * unit, 3 * unit, unit):
        ranges.append([(start, size), (start + size, size)])
        start += 2 * size
    return ranges


def gaps_of(chips):
    bits = bits_of(chips)
    return [
        (d, b) for d in range(chips) for b in bits
        if any(b in children(d, t, bits) for t in range(TREES))
    ]


def gradient_kernel(
    chips, line, scale, made, misfit, grad,
    core_out, core_in, mine, net_out, net_in, own, z_out, z_in,
    core_send, core_recv, net_send, net_recv, z_send, z_recv,
):
    bits = bits_of(chips)
    gaps = gaps_of(chips)
    slices = slices_of(grad.shape[0])
    me = lax.axis_index("blk")
    z = lax.axis_index("narrow")
    chip, core = me // CORES, me % CORES
    other = CORES * chip + 1 - core
    width = made.shape[2]
    part = grad.shape[1]

    barrier = pltpu.get_barrier_semaphore()
    partners = [other] + [CORES * flip(chip, b) + core for b in bits]
    for partner in partners:
        pl.semaphore_signal(barrier, inc=1, device_id={"blk": partner}, device_id_type=MESH)
    beside = [(z + t) % line for t in range(1, line)]
    for partner in beside:
        pl.semaphore_signal(barrier, inc=1, device_id={"narrow": partner}, device_id_type=MESH)

    def term(d, h, c):
        owner = CORES * flip(chip, d) + (core if c == 0 else 1 - core)
        return jnp.dot(misfit[...], made[owner * UNITS + h], preferred_element_type=jnp.float32)

    def span(k):
        start = slices[k][0][0]
        return start, sum(size for _, size in slices[k])

    def across(d, k):
        rows = pl.ds(*span(k))
        return pltpu.make_async_remote_copy(
            core_out.at[d, rows], core_in.at[d, rows], core_send.at[d, k], core_recv.at[d, k],
            device_id={"blk": other}, device_id_type=MESH,
        )

    def compute(into, d, c):
        for h in range(UNITS):
            into[d, :, h * width:(h + 1) * width] = term(d, h, c).astype(into.dtype)

    def net(d, k, t):
        b = toward(d, t)
        start, size = slices[k][t]
        gap = gaps.index((d ^ b, b))
        rows = pl.ds(start, size)
        return pltpu.make_async_remote_copy(
            net_out.at[d - 1, rows], net_in.at[gap, rows],
            net_send.at[d - 1, k, t], net_recv.at[gap, k, t],
            device_id={"blk": CORES * flip(chip, b) + core}, device_id_type=MESH,
        )

    def summed(d, k, t):
        start, size = slices[k][t]
        value = mine[d, start:start + size] + core_in[d, start:start + size].astype(jnp.float32)
        for b in children(d, t, bits):
            gap = gaps.index((d, b))
            rows = pl.ds(start, size)
            pltpu.make_async_remote_copy(
                net_out.at[0, rows], net_in.at[gap, rows],
                net_send.at[0, k, t], net_recv.at[gap, k, t],
                device_id={"blk": other}, device_id_type=MESH,
            ).wait_recv()
            value += net_in[gap, start:start + size].astype(jnp.float32)
        return value

    def pass_on(d, k, t):
        start, size = slices[k][t]
        net_out[d - 1, start:start + size] = summed(d, k, t).astype(jnp.bfloat16)
        net(d, k, t).start()

    away = sorted(((d, t) for d in range(1, chips) for t in range(TREES)), key=lambda p: -ones(p[0]))
    firsts = [p for p in away if not children(*p, bits)]
    relays = [p for p in away if children(*p, bits)]

    def arrive(k):
        for t in range(TREES):
            start, size = slices[k][t]
            value = summed(0, k, t)
            for j in range(line):
                own[j, start:start + size] = value[:, j * part:(j + 1) * part]

    def z_copy(k, t):
        rows = pl.ds(*span(k))
        return pltpu.make_async_remote_copy(
            z_out.at[t - 1, rows], z_in.at[t - 1, rows], z_send.at[t - 1, k], z_recv.at[t - 1, k],
            device_id={"narrow": (z + t) % line}, device_id_type=MESH,
        )

    def spread(k):
        rows = pl.ds(*span(k))
        for t in range(line - 1, 0, -1):
            z_out[t - 1, rows] = own[(z + t) % line, rows].astype(jnp.bfloat16)
            z_copy(k, t).start()

    def finish(k):
        rows = pl.ds(*span(k))
        value = own[z, rows]
        for t in range(1, line):
            z_copy(k, t).wait_recv()
            value += z_in[t - 1, rows].astype(jnp.float32)
        grad[rows] = value * scale

    order = sorted(range(chips), key=lambda d: (-ones(d), d))
    count = len(slices)
    for i, d in enumerate(order):
        compute(core_out, d, 1)
        if i == 0:
            pl.semaphore_wait(barrier, len(partners) + len(beside))
        across(d, 0).start()
    for d in order:
        across(d, 1).start()

    def begin(d, k):
        across(d, k).wait_recv()
        for e, t in firsts:
            if e == d:
                pass_on(d, k, t)

    for d in order:
        compute(mine, d, 0)
        begin(d, 0)
    for now in range(count + 3):
        if now + 2 < count:
            for d in order:
                across(d, now + 2).start()
        if now < count:
            for d, t in relays:
                pass_on(d, now, t)
        if now + 1 < count:
            for d in order:
                begin(d, now + 1)
        if 1 <= now <= count:
            arrive(now - 1)
            spread(now - 1)
        if now >= 3:
            finish(now - 3)

    for k in range(count):
        for d in order:
            across(d, k).wait_send()
        for d, t in away:
            net(d, k, t).wait_send()
        for t in range(1, line):
            z_copy(k, t).wait_send()


def in_hbm(array):
    return pltpu.with_memory_space_constraint(array, pltpu.HBM)


def body(blk, line, codes, signals, dictionary):
    rows, count = codes.shape
    atoms, features = dictionary.shape
    chips = blk // CORES
    width = atoms // UNITS
    blocks = blk * UNITS
    part = atoms // line
    bf16, f32 = jnp.bfloat16, jnp.float32
    hbm_spec = pl.BlockSpec(memory_space=pltpu.HBM)
    vmem_spec = pl.BlockSpec(memory_space=VMEM)
    flops = 2 * rows * count * features
    size = 2 * rows * count

    full, misfit = pl.pallas_call(
        functools.partial(gather_kernel, chips, line),
        out_shape=(
            jax.ShapeDtypeStruct((blocks, features, width), bf16),
            jax.ShapeDtypeStruct((rows, features), bf16),
        ),
        in_specs=[hbm_spec] * 3,
        out_specs=(vmem_spec, vmem_spec),
        scratch_shapes=[
            VMEM((blocks, rows, width), bf16),
            VMEM((rows, features), bf16),
            VMEM((rows, features), f32),
            DMA((blocks,)), DMA, DMA((UNITS,)),
            DMA((UNITS * max(chips - 1, 1),)), DMA((chips, UNITS)), DMA((chips, TREES)),
            DMA((chips, UNITS)), DMA((chips, UNITS)),
        ],
        compiler_params=pltpu.CompilerParams(
            collective_id=0, has_side_effects=True, vmem_limit_bytes=32 * 2**20
        ),
        cost_estimate=pl.CostEstimate(flops=flops, bytes_accessed=2 * size, transcendentals=0),
        name="gather_atoms",
    )(in_hbm(codes), in_hbm(signals), in_hbm(dictionary.T))

    fresh, made, misfit_two = pl.pallas_call(
        functools.partial(update_kernel, 2 * UNITS),
        out_shape=(
            jax.ShapeDtypeStruct((rows, count), bf16),
            jax.ShapeDtypeStruct((blocks, rows, width), bf16),
            jax.ShapeDtypeStruct((features, rows), bf16),
        ),
        in_specs=[vmem_spec] * 4,
        out_specs=(hbm_spec, vmem_spec, vmem_spec),
        scratch_shapes=[
            VMEM((rows, features), f32),
            DMA((blocks,)),
        ],
        compiler_params=pltpu.CompilerParams(vmem_limit_bytes=24 * 2**20),
        cost_estimate=pl.CostEstimate(flops=2 * flops, bytes_accessed=3 * size, transcendentals=0),
        name="update_codes",
    )(codes, signals, full, misfit)

    gaps = max(len(gaps_of(chips)), 1)
    far = max(chips - 1, 1)
    count_of = len(slices_of(features))
    grad = pl.pallas_call(
        functools.partial(gradient_kernel, chips, line, float(rows * blk * line) ** -0.5),
        out_shape=jax.ShapeDtypeStruct((features, part), f32),
        in_specs=[vmem_spec] * 2,
        out_specs=vmem_spec,
        scratch_shapes=[
            VMEM((chips, features, atoms), bf16),
            VMEM((chips, features, atoms), bf16),
            VMEM((chips, features, atoms), f32),
            VMEM((far, features, atoms), bf16),
            VMEM((gaps, features, atoms), bf16),
            VMEM((line, features, part), f32),
            VMEM((max(line - 1, 1), features, part), bf16),
            VMEM((max(line - 1, 1), features, part), bf16),
            DMA((chips, count_of)), DMA((chips, count_of)),
            DMA((far, count_of, TREES)), DMA((gaps, count_of, TREES)),
            DMA((max(line - 1, 1), count_of)), DMA((max(line - 1, 1), count_of)),
        ],
        compiler_params=pltpu.CompilerParams(
            collective_id=1, has_side_effects=True, vmem_limit_bytes=32 * 2**20
        ),
        cost_estimate=pl.CostEstimate(flops=flops, bytes_accessed=2 * size, transcendentals=0),
        name="dictionary_gradient",
    )(made, misfit_two)
    return fresh, grad.T


def solution(mesh):
    placed = (P(("blk", "narrow"), None), P(("blk", "narrow"), None), P("blk", None))
    return jax.shard_map(
        functools.partial(body, mesh.shape["blk"], mesh.shape["narrow"]),
        mesh=mesh,
        in_specs=placed,
        out_specs=(P(("blk", "narrow"), None), P(("blk", "narrow"), None)),
        check_vma=False,
    )
```
